256 devices in a mesh: vel: 32 (over y, x, core), grp: 8 (over z).
Axes of the slice: x: 4, y: 4, z: 8, core: 2. Of those that a mesh axis runs over, the one named last changes fastest.
Arguments:
- adjoint: bfloat16 [512, 8, 32, 2048], P('vel', 'grp'), may hold values from -33 to 33
- relaxation: float32 [8, 32, 2048], P('grp', 'vel'), may hold values from 0.6 to 1.9
- reaction: float32 [8, 32, 2048], P('grp', 'vel'), may hold values from 0.05 to 0.6
- base_moments: float32 [10, 8, 32, 2048], P(None, 'grp', 'vel'), may hold values from -6 to 6
- cell_kind: int32 [8, 32, 2048], P('grp', 'vel'), may hold values from 0 to 2
- patch_id: int32 [8, 32, 2048], P('grp', 'vel'), may hold values from 0 to 4095, as said below
Outputs:
- adjoint_out: bfloat16 [512, 8, 32, 2048], P(None, 'grp', 'vel')
- patch_grad: float32 [4096], P(('vel', 'grp'))
The draws below stay inside these ranges and needn't reach their ends.
Inputs may be any that keep to these rules, and one draw needn't show every extreme that they name: For a voxel of layer g * 32 + l, (patch_id // 16) % 8 equals g.
All inputs are finite; a program needn't handle non-finite values.
Results may differ from the reference program's by a relative error of at most 0.0036.
Values may be sent and summed in bfloat16 or wider, within the bound.
A program may use at most 128 MiB of HBM per device.

```python
import math
import jax
import jax.numpy as jnp
from jax import lax

NV = 8
MOMENTS = 10
PY = 16
PZ = 128
PATCH_DEV = 16
Q = 512
XB = 32
NXG = 8
NX = 256
NP = 4096


def component_drawn(grid_digit):
    signed = jnp.where(grid_digit % 2 == 0, -1.0, 1.0).astype(jnp.float32)
    return signed * ((grid_digit // 2).astype(jnp.float32) + 0.5) / (NV / 2.0 - 0.5)


def draw_adjoint(key, part):
    noise_key = jax.random.fold_in(key, 11)
    field_key = jax.random.fold_in(key, 12)
    shape_all = (Q, NXG, XB, PY * PZ)
    vel_index = jnp.arange(Q, dtype=jnp.int32)
    column = (Q, 1, 1, 1)
    vel_x = component_drawn(vel_index % NV).reshape(column)
    vel_y = component_drawn(vel_index // NV % NV).reshape(column)
    vel_z = component_drawn(vel_index // (NV * NV)).reshape(column)
    noise_part = jax.random.truncated_normal(noise_key, -4.0, 4.0, shape_all, jnp.float32)
    fields = jax.random.truncated_normal(field_key, -4.0, 4.0, (4, NXG, XB, PY * PZ), jnp.float32)
    strength = 1.5
    mixed = noise_part + strength * (fields[0] + fields[1] * vel_x + fields[2] * vel_y + fields[3] * (vel_z * vel_z - 1.0 / 3.0))
    return mixed.astype(jnp.bfloat16)


def draw_cell_kind(key, part):
    shape_all = (NXG, XB, PY * PZ)
    layer = lax.broadcasted_iota(jnp.int32, shape_all, 0) * XB + lax.broadcasted_iota(jnp.int32, shape_all, 1)
    wall_share = 16 + 160 * (layer * 7 % 13) // 12
    draws = jax.random.randint(key, shape_all, 0, 256, dtype=jnp.int32)
    return jnp.where(draws < 48, 0, jnp.where(draws < 48 + wall_share, 2, 1)).astype(jnp.int32)


def draw_patch_id(key, part):
    shape_all = (NXG, XB, PY * PZ)
    slot = jax.random.randint(jax.random.fold_in(key, 21), shape_all, 0, PATCH_DEV * XB, dtype=jnp.int32)
    group_index = lax.broadcasted_iota(jnp.int32, shape_all, 0)
    return ((slot // PATCH_DEV * NXG + group_index) * PATCH_DEV + slot % PATCH_DEV).astype(jnp.int32)


def shard_levels(own_key, extent, cuts, low, top_value):
    factor_of = 1.0
    for dim, parts in cuts:
        heights = jax.random.uniform(jax.random.fold_in(jax.random.fold_in(own_key, 6), dim), (parts,), jnp.float32, low / len(cuts), top_value / len(cuts))
        factor_of = factor_of * jnp.repeat(jnp.exp(heights), extent[dim] // parts).reshape((-1,) + (1,) * (len(extent) - 1 - dim))
    return factor_of


def noise(key, shape, width, most, pieces=(), kind=jnp.bfloat16):
    entries = width * jax.random.normal(key, shape, jnp.float32)
    if pieces:
        entries = entries * shard_levels(key, shape, pieces, -0.22, 0.18)
    return jnp.clip(entries, -most, most).astype(kind)


def setup_inputs(seed: int = 0) -> dict:
    keys = jax.random.split(jax.random.key(seed), 7)
    adjoint = draw_adjoint(jax.random.fold_in(keys[6], 71), 0)
    relaxation = jnp.clip(jnp.exp(math.log(1.9) - 1.1526795 * jax.random.uniform(keys[1], (NXG, XB, PY * PZ), jnp.float32) ** shard_levels(keys[1], (NXG, XB, PY * PZ), ((0, 8), (1, 32)), -0.2, 0.2)), 0.6, 1.9)
    reaction = jnp.clip(jnp.exp(math.log(0.6) - 2.4849067 * jax.random.uniform(keys[2], (NXG, XB, PY * PZ), jnp.float32) ** shard_levels(keys[2], (NXG, XB, PY * PZ), ((0, 8), (1, 32)), -0.2, 0.2)), 0.05, 0.6)
    base_moments = noise(keys[3], (MOMENTS, NXG, XB, PY * PZ), 1.0, 6.0, ((1, 8), (2, 32)), jnp.float32)
    cell_kind = draw_cell_kind(jax.random.fold_in(keys[6], 71), 0)
    patch_id = draw_patch_id(jax.random.fold_in(keys[6], 71), 0)
    return dict(adjoint=adjoint, relaxation=relaxation, reaction=reaction, base_moments=base_moments, cell_kind=cell_kind, patch_id=patch_id)


courant = 0.3


def component(grid_digit):
    signed = jnp.where(grid_digit % 2 == 0, -1.0, 1.0).astype(jnp.float32)
    return signed * ((grid_digit // 2).astype(jnp.float32) + 0.5) / (NV / 2.0 - 0.5)


def velocities(vel_index):
    return (component(vel_index % NV), component((vel_index // NV) % NV), component(vel_index // (NV * NV)))


def moment_basis(vel_x, vel_y, vel_z):
    third_part = 1.0 / 3.0
    return jnp.stack([jnp.ones_like(vel_x), vel_x, vel_y, vel_z, vel_x * vel_x - third_part, vel_y * vel_y - third_part, vel_z * vel_z - third_part, vel_x * vel_y, vel_x * vel_z, vel_y * vel_z])


def advect_block(field_block, vel_x, vel_y, vel_z):
    shape_col = (-1, 1, 1, 1)
    padded = jnp.pad(field_block, ((0, 0), (1, 1), (0, 0), (0, 0)))
    along_x = jnp.where(vel_x.reshape(shape_col) > 0, padded[:, 2:], padded[:, :-2])
    along_y = jnp.where(vel_y.reshape(shape_col) > 0, jnp.roll(field_block, -1, 2), jnp.roll(field_block, 1, 2))
    along_z = jnp.where(vel_z.reshape(shape_col) > 0, jnp.roll(field_block, -1, 3), jnp.roll(field_block, 1, 3))
    rate_x = courant * jnp.abs(vel_x).reshape(shape_col)
    rate_y = courant * jnp.abs(vel_y).reshape(shape_col)
    rate_z = courant * jnp.abs(vel_z).reshape(shape_col)
    mixed = (1.0 - rate_x - rate_y - rate_z) * field_block + rate_x * along_x + rate_y * along_y + rate_z * along_z
    return mixed.astype(jnp.bfloat16)


def reference(adjoint, relaxation, reaction, base_moments, cell_kind, patch_id):
    vel_index = jnp.arange(Q, dtype=jnp.int32)
    vel_x, vel_y, vel_z = velocities(vel_index)
    grouped = adjoint.reshape(NV, NV * NV, NX, PY, PZ)

    def advect_group(block_items):
        return advect_block(block_items[0].astype(jnp.float32), block_items[1], block_items[2], block_items[3])

    advected = lax.map(advect_group, (grouped, vel_x.reshape(NV, NV * NV), vel_y.reshape(NV, NV * NV), vel_z.reshape(NV, NV * NV)))
    mu_wide = advected.reshape(Q, NX * PY * PZ).astype(jnp.float32)
    poly_basis = moment_basis(vel_x, vel_y, vel_z)
    speed_sq = vel_x * vel_x + vel_y * vel_y + vel_z * vel_z
    weight = jnp.exp(-speed_sq)
    absorb = speed_sq / 3.0
    total_weight = jnp.sum(weight)
    etable = jnp.concatenate([poly_basis * weight, poly_basis * (weight * absorb)], axis=0)
    projected = jnp.dot(etable, mu_wide, precision=lax.Precision.HIGHEST)
    kind_flat = cell_kind.reshape(-1)
    is_wall = kind_flat == 2
    fluid_mask = jnp.where(kind_flat != 0, 1.0, 0.0).astype(jnp.float32)
    wall_rate = jnp.where(is_wall, reaction.reshape(-1), 0.0).astype(jnp.float32)
    moments = (projected[:MOMENTS] - wall_rate * projected[MOMENTS:]) / total_weight
    relax_rate = relaxation.reshape(-1)
    collided = jnp.dot(poly_basis.T, moments, precision=lax.Precision.HIGHEST)
    damped = (1.0 - wall_rate * absorb[:, None]) * mu_wide
    adjoint_out = (fluid_mask * ((1.0 - relax_rate) * damped + relax_rate * collided)).astype(jnp.bfloat16)
    sensitivity = -wall_rate * jnp.sum(base_moments.reshape(MOMENTS, -1) * projected[MOMENTS:], axis=0) / total_weight
    patch_grad = jax.ops.segment_sum(sensitivity, patch_id.reshape(-1).astype(jnp.int32), num_segments=NP)
    return adjoint_out.reshape(Q, NXG, XB, PY * PZ), patch_grad
```

```python
import jax
import jax.numpy as jnp
from jax import lax
from jax.experimental import pallas as pl
from jax.experimental.pallas import tpu as pltpu
from jax.sharding import PartitionSpec as P

NV = 8
MOMENTS = 10
PY = 16
PZ = 128
PATCH_DEV = 16
Q = 512
XB = 32
CELLS = PY * PZ
COURANT = 0.3

VEL = 32
GRP = 8
LOCAL = Q // VEL
CHUNKS = 4
WIDTH = CELLS // CHUNKS
ROWS = 128
STEP = 13

MESH = pl.DeviceIdType.MESH
F32 = jnp.float32
BF16 = jnp.bfloat16


def component(digit):
    sign = jnp.where((digit & 1) == 0, -1.0, 1.0).astype(F32)
    return sign * ((digit >> 1).astype(F32) + 0.5) / (NV / 2.0 - 0.5)


def velocities(vel_index):
    return (
        component(vel_index & (NV - 1)),
        component((vel_index >> 3) & (NV - 1)),
        component(vel_index >> 6),
    )


def poly(k, ux, uy, uz):
    third = 1.0 / 3.0
    terms = (
        jnp.ones_like(ux),
        ux,
        uy,
        uz,
        ux * ux - third,
        uy * uy - third,
        uz * uz - third,
        ux * uy,
        ux * uz,
        uy * uz,
    )
    value = jnp.zeros_like(ux)
    for i, term in enumerate(terms):
        value = jnp.where(k == i, term, value)
    return value


def split(value):
    high = value.astype(BF16)
    return high, (value - high.astype(F32)).astype(BF16)


def kernel(
    adj_hbm, relax_hbm, react_hbm, base_hbm, kind_hbm, patch_hbm,
    out_hbm, grad_out,
    xin, turned, staged, mu, result, relax, react, base, kind, patch,
    absorb_tab, etab, btab, part, part_in, total,
    load_sem, small_sem, halo_send, halo_recv, send_sem, recv_sem, out_sem, psend_sem, precv_sem,
):
    v = lax.axis_index("vel")
    g = lax.axis_index("grp")
    core = v & 1

    load = pltpu.make_async_copy(adj_hbm.at[:, 0], xin, load_sem)
    load.start()
    smalls = [
        pltpu.make_async_copy(relax_hbm.at[0], relax, small_sem.at[0]),
        pltpu.make_async_copy(react_hbm.at[0], react, small_sem.at[1]),
        pltpu.make_async_copy(kind_hbm.at[0], kind, small_sem.at[2]),
        pltpu.make_async_copy(patch_hbm.at[0], patch, small_sem.at[3]),
        pltpu.make_async_copy(base_hbm.at[:, 0], base, small_sem.at[4]),
    ]
    for copy in smalls:
        copy.start()

    barrier = pltpu.get_barrier_semaphore()

    def greet(k, _):
        pl.semaphore_signal(barrier, inc=1, device_id={"vel": (v + k) & (VEL - 1)}, device_id_type=MESH)
        return 0

    lax.fori_loop(1, VEL, greet, 0)

    @pl.when(g > 0)
    def _():
        pl.semaphore_signal(barrier, inc=1, device_id={"grp": g - 1}, device_id_type=MESH)

    @pl.when(g < GRP - 1)
    def _():
        pl.semaphore_signal(barrier, inc=1, device_id={"grp": g + 1}, device_id_type=MESH)

    row = lax.broadcasted_iota(jnp.int32, (256, 256), 0)
    col = lax.broadcasted_iota(jnp.int32, (256, 256), 1)
    perm = jnp.where(col == ((row & 15) << 4) + (row >> 4), 1.0, 0.0).astype(BF16)
    load.wait()
    for t in range(2):
        for c in range(CHUNKS):
            cols = pl.ds(c * WIDTH, WIDTH)
            block = xin[:, pl.ds(16 * t, 16), cols].reshape(256, WIDTH)
            moved = jnp.dot(perm, block, preferred_element_type=F32).astype(BF16)
            turned[pl.ds(1 + 16 * t, 16), :, cols] = moved.reshape(16, LOCAL, WIDTH)

    neighbours = jnp.where(g > 0, 1, 0) + jnp.where(g < GRP - 1, 1, 0)
    pl.semaphore_wait(barrier, VEL - 1 + neighbours)

    def to_lower():
        return pltpu.make_async_remote_copy(
            src_ref=turned.at[1], dst_ref=turned.at[XB + 1], send_sem=halo_send.at[0], recv_sem=halo_recv.at[0],
            device_id={"grp": g - 1}, device_id_type=MESH,
        )

    def to_upper():
        return pltpu.make_async_remote_copy(
            src_ref=turned.at[XB], dst_ref=turned.at[0], send_sem=halo_send.at[1], recv_sem=halo_recv.at[1],
            device_id={"grp": g + 1}, device_id_type=MESH,
        )

    @pl.when(g > 0)
    def _():
        to_lower().start()

    @pl.when(g < GRP - 1)
    def _():
        to_upper().start()

    @pl.when(g == 0)
    def _():
        turned[0] = jnp.zeros((LOCAL, CELLS), BF16)

    @pl.when(g == GRP - 1)
    def _():
        turned[XB + 1] = jnp.zeros((LOCAL, CELLS), BF16)

    own = v * LOCAL + lax.broadcasted_iota(jnp.int32, (LOCAL, PZ), 0)
    ux, uy, uz = velocities(own)
    rate_x, rate_y, rate_z = COURANT * jnp.abs(ux), COURANT * jnp.abs(uy), COURANT * jnp.abs(uz)
    rest = 1.0 - rate_x - rate_y - rate_z
    forward_x = ux > 0
    half = LOCAL // 2
    shift_z = jnp.where(((v >> 2) & 1) == 1, PZ - 1, 1)

    def advect(layer, c, store):
        count = WIDTH // PZ

        def cells(at, j):
            return turned[at, :, pl.ds((j % PY) * PZ, PZ)].astype(F32)

        centre = [cells(layer + 1, c * count + j) for j in range(-1, count + 1)]
        for j in range(count):
            block = centre[j + 1]
            along_x = jnp.where(forward_x, cells(layer + 2, c * count + j), cells(layer, c * count + j))
            along_y = jnp.concatenate([centre[j][:half], centre[j + 2][half:]], axis=0)
            along_z = pltpu.roll(block, shift_z, 1)
            value = rest * block + rate_x * along_x + rate_y * along_y + rate_z * along_z
            store(pl.ds((c * count + j) * PZ, PZ), value.astype(BF16))

    def target(k):
        o = (k * STEP) & (VEL - 1)
        da, db, dc = (o >> 1) & 3, o >> 3, o & 1
        dx = jnp.where(core == 0, da, db)
        dy = jnp.where(core == 0, db, da)
        y, x = v >> 3, (v >> 1) & 3
        return (((y + dy) & 3) << 3) + (((x + dx) & 3) << 1) + ((core + dc) & 1)

    own_rows = pl.ds(pl.multiple_of(v * LOCAL, LOCAL), LOCAL)

    def advect_and_send(layer, c):
        cols = pl.ds(c * WIDTH, WIDTH)

        def store(at, value):
            staged[layer, :, at] = value

        advect(layer, c, store)
        pltpu.make_async_remote_copy(
            src_ref=staged.at[layer, :, cols], dst_ref=mu.at[own_rows, cols], send_sem=send_sem, recv_sem=recv_sem.at[c],
            device_id={"vel": layer}, device_id_type=MESH,
        ).start()

    for c in range(CHUNKS):

        def step(k, _):
            layer = target(k)
            if c == 0:

                @pl.when((layer > 0) & (layer < XB - 1))
                def _():
                    advect_and_send(layer, c)
            else:
                advect_and_send(layer, c)
            return 0

        lax.fori_loop(1, VEL, step, 0)
        if c == 0:

            @pl.when(g > 0)
            def _():
                to_upper().wait_recv()

            @pl.when(g < GRP - 1)
            def _():
                to_lower().wait_recv()

            for layer in (0, XB - 1):

                @pl.when(v != layer)
                def _():
                    advect_and_send(layer, 0)

    def store_own(at, value):
        mu[own_rows, at] = value

    for c in range(CHUNKS):
        advect(v, c, store_own)

    q_row = lax.broadcasted_iota(jnp.int32, (64, Q), 1)
    j_row = lax.broadcasted_iota(jnp.int32, (64, Q), 0)
    ux, uy, uz = velocities(q_row)
    speed = ux * ux + uy * uy + uz * uz
    weight = jnp.exp(-speed)
    total_weight = jnp.sum(weight[0:8], axis=1, keepdims=True)[0:1]
    entry = poly(j_row & 15, ux, uy, uz) * jnp.where((j_row & 16) == 0, weight, weight * (speed / 3.0))
    high = entry.astype(BF16).astype(F32)
    etab[...] = jnp.where(j_row < 32, high, entry - high).astype(BF16)

    for r in range(Q // ROWS):
        rows = pl.ds(r * ROWS, ROWS)
        q_col = r * ROWS + lax.broadcasted_iota(jnp.int32, (ROWS, 128), 0)
        j_col = lax.broadcasted_iota(jnp.int32, (ROWS, 128), 1)
        ux, uy, uz = velocities(q_col)
        absorb_tab[rows, :] = (ux * ux + uy * uy + uz * uz) / 3.0
        entry = poly(j_col & 15, ux, uy, uz)
        high = entry.astype(BF16).astype(F32)
        btab[rows, :] = jnp.where((j_col & 16) == 0, high, entry - high).astype(BF16)

    for copy in smalls:
        copy.wait()

    total[...] = jnp.zeros((VEL, 128), F32)
    for c in range(CHUNKS):
        cols = pl.ds(c * WIDTH, WIDTH)
        arrived = mu.at[pl.ds(0, (VEL - 1) * LOCAL), cols]
        pltpu.make_async_copy(arrived, arrived, recv_sem.at[c]).wait()
        product = jnp.dot(etab[...], mu[:, cols], preferred_element_type=F32)
        first = product[0:16] + product[32:48]
        second = product[16:32] + product[48:64]
        kind_c = kind[:, cols]
        wall = jnp.where(kind_c == 2, react[:, cols], 0.0)
        fluid = jnp.where(kind_c != 0, 1.0, 0.0)
        relax_c = relax[:, cols]

        acc = base[0, :, cols] * second[0:1]
        for k in range(1, MOMENTS):
            acc = acc + base[k, :, cols] * second[k : k + 1]
        sens = -wall * acc / total_weight
        patch_c = patch[:, cols]
        owner = lax.broadcasted_iota(jnp.int32, (VEL, WIDTH), 0) == (patch_c >> 7)
        spread = jnp.where(owner, sens, 0.0)
        piece0 = spread.astype(BF16)
        left = spread - piece0.astype(F32)
        piece1 = left.astype(BF16)
        piece2 = (left - piece1.astype(F32)).astype(BF16)
        slot = lax.broadcasted_iota(jnp.int32, (128, WIDTH), 0) == (patch_c & 15)
        sums = lax.dot_general(
            jnp.concatenate([piece0, piece1, piece2], axis=0),
            jnp.where(slot, 1.0, 0.0).astype(BF16),
            (((1,), (1,)), ((), ())),
            preferred_element_type=F32,
        )
        total[...] += sums[0:VEL] + sums[VEL : 2 * VEL] + sums[2 * VEL :]
        if c == CHUNKS - 1:
            for i in range(VEL):
                part[i] = total[i : i + 1]

            def give(k, _):
                owner = target(k)
                pltpu.make_async_remote_copy(
                    src_ref=part.at[owner], dst_ref=part_in.at[v], send_sem=psend_sem, recv_sem=precv_sem,
                    device_id={"vel": owner}, device_id_type=MESH,
                ).start()
                return 0

            lax.fori_loop(1, VEL, give, 0)

        moments = (fluid * relax_c) * ((first - wall * second) / total_weight)
        high, low = split(moments)
        stacked = jnp.concatenate([high, high, low, low], axis=0)
        keep = fluid * (1.0 - relax_c)
        keep_wall = keep * wall
        for r in range(Q // ROWS):
            rows = pl.ds(r * ROWS, ROWS)
            collided = jnp.dot(btab[rows, 0:64], stacked, preferred_element_type=F32)
            for j in range(WIDTH // 128):
                sub = slice(j * 128, (j + 1) * 128)
                at = pl.ds(c * WIDTH + j * 128, 128)
                factor = keep[:, sub] - keep_wall[:, sub] * absorb_tab[rows, :]
                value = factor * mu[rows, at].astype(F32) + collided[:, sub]
                result[rows, at] = value.astype(BF16)
        pltpu.make_async_copy(result.at[:, cols], out_hbm.at[:, cols], out_sem.at[c]).start()

    part_in[pl.ds(v, 1)] = part[pl.ds(v, 1)]
    sent = part.at[pl.ds(0, VEL - 1)]
    pltpu.make_async_copy(sent, sent, precv_sem).wait()
    grad = part_in[0]
    for i in range(1, VEL):
        grad = grad + part_in[i]
    grad_out[...] = grad

    pltpu.make_async_copy(sent, sent, psend_sem).wait()
    staged_out = staged.at[pl.ds(0, VEL - 1)]
    pltpu.make_async_copy(staged_out, staged_out, send_sem).wait()

    @pl.when(g > 0)
    def _():
        to_lower().wait_send()

    @pl.when(g < GRP - 1)
    def _():
        to_upper().wait_send()

    for c in range(CHUNKS):
        cols = pl.ds(c * WIDTH, WIDTH)
        pltpu.make_async_copy(result.at[:, cols], out_hbm.at[:, cols], out_sem.at[c]).wait()


def body(adjoint, relaxation, reaction, base_moments, cell_kind, patch_id):
    anywhere = pl.BlockSpec(memory_space=pl.ANY)
    dma = pltpu.SemaphoreType.DMA
    out, grad = pl.pallas_call(
        kernel,
        out_shape=(jax.ShapeDtypeStruct((Q, CELLS), BF16), jax.ShapeDtypeStruct((1, 128), F32)),
        in_specs=[anywhere] * 6,
        out_specs=(anywhere, pl.BlockSpec(memory_space=pltpu.VMEM)),
        scratch_shapes=[
            pltpu.VMEM((LOCAL, XB, CELLS), BF16),
            pltpu.VMEM((XB + 2, LOCAL, CELLS), BF16),
            pltpu.VMEM((XB, LOCAL, CELLS), BF16),
            pltpu.VMEM((Q, CELLS), BF16),
            pltpu.VMEM((Q, CELLS), BF16),
            pltpu.VMEM((1, CELLS), F32),
            pltpu.VMEM((1, CELLS), F32),
            pltpu.VMEM((MOMENTS, 1, CELLS), F32),
            pltpu.VMEM((1, CELLS), jnp.int32),
            pltpu.VMEM((1, CELLS), jnp.int32),
            pltpu.VMEM((Q, 128), F32),
            pltpu.VMEM((64, Q), BF16),
            pltpu.VMEM((Q, 128), BF16),
            pltpu.VMEM((VEL, 1, 128), F32),
            pltpu.VMEM((VEL, 1, 128), F32),
            pltpu.VMEM((VEL, 128), F32),
            dma,
            dma((5,)),
            dma((2,)),
            dma((2,)),
            dma,
            dma((CHUNKS,)),
            dma((CHUNKS,)),
            dma,
            dma,
        ],
        compiler_params=pltpu.CompilerParams(
            collective_id=0, has_side_effects=True, vmem_limit_bytes=60 * 1024 * 1024
        ),
        name="adjoint_step",
    )(adjoint, relaxation, reaction, base_moments, cell_kind, patch_id)
    return out.reshape(Q, 1, 1, CELLS), grad[0, :PATCH_DEV]


def solution(mesh):
    placed = (
        P("vel", "grp", None, None),
        P("grp", "vel", None),
        P("grp", "vel", None),
        P(None, "grp", "vel", None),
        P("grp", "vel", None),
        P("grp", "vel", None),
    )
    return jax.shard_map(
        body,
        mesh=mesh,
        in_specs=placed,
        out_specs=(P(None, "grp", "vel", None), P(("vel", "grp"))),
        check_vma=False,
    )
```

```python
import jax
import jax.numpy as jnp
from jax import lax
from jax.experimental import pallas as pl
from jax.experimental.pallas import tpu as pltpu
from jax.sharding import PartitionSpec as P

NV = 8
MOMENTS = 10
PY = 16
PZ = 128
PATCH_DEV = 16
Q = 512
XB = 32
CELLS = PY * PZ
COURANT = 0.3

VEL = 32
GRP = 8
LOCAL = Q // VEL
CHUNKS = 4
WIDTH = CELLS // CHUNKS
ROWS = 128
STEP = 13

MESH = pl.DeviceIdType.MESH
F32 = jnp.float32
BF16 = jnp.bfloat16


def component(digit):
    sign = jnp.where((digit & 1) == 0, -1.0, 1.0).astype(F32)
    return sign * ((digit >> 1).astype(F32) + 0.5) / (NV / 2.0 - 0.5)


def velocities(vel_index):
    return (
        component(vel_index & (NV - 1)),
        component((vel_index >> 3) & (NV - 1)),
        component(vel_index >> 6),
    )


def poly(k, ux, uy, uz):
    third = 1.0 / 3.0
    terms = (
        jnp.ones_like(ux),
        ux,
        uy,
        uz,
        ux * ux - third,
        uy * uy - third,
        uz * uz - third,
        ux * uy,
        ux * uz,
        uy * uz,
    )
    value = jnp.zeros_like(ux)
    for i, term in enumerate(terms):
        value = jnp.where(k == i, term, value)
    return value


def split(value):
    high = value.astype(BF16)
    return high, (value - high.astype(F32)).astype(BF16)


def kernel(
    adj_hbm, relax_hbm, react_hbm, base_hbm, kind_hbm, patch_hbm,
    result, grad_out,
    xin, turned, staged, mu, relax, react, base, kind, patch,
    absorb_tab, etab, btab, part, part_in, total,
    load_sem, small_sem, halo_send, halo_recv, send_sem, recv_sem, psend_sem, precv_sem,
):
    v = lax.axis_index("vel")
    g = lax.axis_index("grp")
    core = v & 1

    load = pltpu.make_async_copy(adj_hbm.at[:, 0], xin, load_sem)
    load.start()
    smalls = [
        pltpu.make_async_copy(relax_hbm.at[0], relax, small_sem.at[0]),
        pltpu.make_async_copy(react_hbm.at[0], react, small_sem.at[1]),
        pltpu.make_async_copy(kind_hbm.at[0], kind, small_sem.at[2]),
        pltpu.make_async_copy(patch_hbm.at[0], patch, small_sem.at[3]),
        pltpu.make_async_copy(base_hbm.at[:, 0], base, small_sem.at[4]),
    ]
    for copy in smalls:
        copy.start()

    barrier = pltpu.get_barrier_semaphore()

    def greet(k, _):
        pl.semaphore_signal(barrier, inc=1, device_id={"vel": (v + k) & (VEL - 1)}, device_id_type=MESH)
        return 0

    lax.fori_loop(1, VEL, greet, 0)

    @pl.when(g > 0)
    def _():
        pl.semaphore_signal(barrier, inc=1, device_id={"grp": g - 1}, device_id_type=MESH)

    @pl.when(g < GRP - 1)
    def _():
        pl.semaphore_signal(barrier, inc=1, device_id={"grp": g + 1}, device_id_type=MESH)

    row = lax.broadcasted_iota(jnp.int32, (256, 256), 0)
    col = lax.broadcasted_iota(jnp.int32, (256, 256), 1)
    perm = jnp.where(col == ((row & 15) << 4) + (row >> 4), 1.0, 0.0).astype(BF16)
    load.wait()
    for t in range(2):
        for c in range(CHUNKS):
            cols = pl.ds(c * WIDTH, WIDTH)
            block = xin[:, pl.ds(16 * t, 16), cols].reshape(256, WIDTH)
            moved = jnp.dot(perm, block, preferred_element_type=F32).astype(BF16)
            turned[pl.ds(1 + 16 * t, 16), :, cols] = moved.reshape(16, LOCAL, WIDTH)

    neighbours = jnp.where(g > 0, 1, 0) + jnp.where(g < GRP - 1, 1, 0)
    pl.semaphore_wait(barrier, VEL - 1 + neighbours)

    def to_lower():
        return pltpu.make_async_remote_copy(
            src_ref=turned.at[1], dst_ref=turned.at[XB + 1], send_sem=halo_send.at[0], recv_sem=halo_recv.at[0],
            device_id={"grp": g - 1}, device_id_type=MESH,
        )

    def to_upper():
        return pltpu.make_async_remote_copy(
            src_ref=turned.at[XB], dst_ref=turned.at[0], send_sem=halo_send.at[1], recv_sem=halo_recv.at[1],
            device_id={"grp": g + 1}, device_id_type=MESH,
        )

    @pl.when(g > 0)
    def _():
        to_lower().start()

    @pl.when(g < GRP - 1)
    def _():
        to_upper().start()

    @pl.when(g == 0)
    def _():
        turned[0] = jnp.zeros((LOCAL, CELLS), BF16)

    @pl.when(g == GRP - 1)
    def _():
        turned[XB + 1] = jnp.zeros((LOCAL, CELLS), BF16)

    own = v * LOCAL + lax.broadcasted_iota(jnp.int32, (LOCAL, PZ), 0)
    ux, uy, uz = velocities(own)
    rate_x, rate_y, rate_z = COURANT * jnp.abs(ux), COURANT * jnp.abs(uy), COURANT * jnp.abs(uz)
    rest = 1.0 - rate_x - rate_y - rate_z
    forward_x = ux > 0
    half = LOCAL // 2
    shift_z = jnp.where(((v >> 2) & 1) == 1, PZ - 1, 1)

    def advect(layer, c, store):
        count = WIDTH // PZ

        def cells(at, j):
            return turned[at, :, pl.ds((j % PY) * PZ, PZ)].astype(F32)

        centre = [cells(layer + 1, c * count + j) for j in range(-1, count + 1)]
        for j in range(count):
            block = centre[j + 1]
            along_x = jnp.where(forward_x, cells(layer + 2, c * count + j), cells(layer, c * count + j))
            along_y = jnp.concatenate([centre[j][:half], centre[j + 2][half:]], axis=0)
            along_z = pltpu.roll(block, shift_z, 1)
            value = rest * block + rate_x * along_x + rate_y * along_y + rate_z * along_z
            store(pl.ds((c * count + j) * PZ, PZ), value.astype(BF16))

    def target(k):
        o = (k * STEP) & (VEL - 1)
        da, db, dc = (o >> 1) & 3, o >> 3, o & 1
        dx = jnp.where(core == 0, da, db)
        dy = jnp.where(core == 0, db, da)
        y, x = v >> 3, (v >> 1) & 3
        return (((y + dy) & 3) << 3) + (((x + dx) & 3) << 1) + ((core + dc) & 1)

    own_rows = pl.ds(pl.multiple_of(v * LOCAL, LOCAL), LOCAL)

    def advect_and_send(layer, c):
        cols = pl.ds(c * WIDTH, WIDTH)

        def store(at, value):
            staged[layer, :, at] = value

        advect(layer, c, store)
        pltpu.make_async_remote_copy(
            src_ref=staged.at[layer, :, cols], dst_ref=mu.at[own_rows, cols], send_sem=send_sem, recv_sem=recv_sem.at[c],
            device_id={"vel": layer}, device_id_type=MESH,
        ).start()

    for c in range(CHUNKS):

        def step(k, _):
            layer = target(k)
            if c == 0:

                @pl.when((layer > 0) & (layer < XB - 1))
                def _():
                    advect_and_send(layer, c)
            else:
                advect_and_send(layer, c)
            return 0

        lax.fori_loop(1, VEL, step, 0)
        if c == 0:

            @pl.when(g > 0)
            def _():
                to_upper().wait_recv()

            @pl.when(g < GRP - 1)
            def _():
                to_lower().wait_recv()

            for layer in (0, XB - 1):

                @pl.when(v != layer)
                def _():
                    advect_and_send(layer, 0)

    def store_own(at, value):
        mu[own_rows, at] = value

    for c in range(CHUNKS):
        advect(v, c, store_own)

    q_row = lax.broadcasted_iota(jnp.int32, (64, Q), 1)
    j_row = lax.broadcasted_iota(jnp.int32, (64, Q), 0)
    ux, uy, uz = velocities(q_row)
    speed = ux * ux + uy * uy + uz * uz
    weight = jnp.exp(-speed)
    total_weight = jnp.sum(weight[0:8], axis=1, keepdims=True)[0:1]
    entry = poly(j_row & 15, ux, uy, uz) * jnp.where((j_row & 16) == 0, weight, weight * (speed / 3.0))
    high = entry.astype(BF16).astype(F32)
    etab[...] = jnp.where(j_row < 32, high, entry - high).astype(BF16)

    for r in range(Q // ROWS):
        rows = pl.ds(r * ROWS, ROWS)
        q_col = r * ROWS + lax.broadcasted_iota(jnp.int32, (ROWS, 128), 0)
        j_col = lax.broadcasted_iota(jnp.int32, (ROWS, 128), 1)
        ux, uy, uz = velocities(q_col)
        absorb_tab[rows, :] = (ux * ux + uy * uy + uz * uz) / 3.0
        entry = poly(j_col & 15, ux, uy, uz)
        high = entry.astype(BF16).astype(F32)
        btab[rows, :] = jnp.where((j_col & 16) == 0, high, entry - high).astype(BF16)

    for copy in smalls:
        copy.wait()

    total[...] = jnp.zeros((VEL, 128), F32)
    for c in range(CHUNKS):
        cols = pl.ds(c * WIDTH, WIDTH)
        arrived = mu.at[pl.ds(0, (VEL - 1) * LOCAL), cols]
        pltpu.make_async_copy(arrived, arrived, recv_sem.at[c]).wait()
        product = jnp.dot(etab[...], mu[:, cols], preferred_element_type=F32)
        first = product[0:16] + product[32:48]
        second = product[16:32] + product[48:64]
        kind_c = kind[:, cols]
        wall = jnp.where(kind_c == 2, react[:, cols], 0.0)
        fluid = jnp.where(kind_c != 0, 1.0, 0.0)
        relax_c = relax[:, cols]

        acc = base[0, :, cols] * second[0:1]
        for k in range(1, MOMENTS):
            acc = acc + base[k, :, cols] * second[k : k + 1]
        sens = -wall * acc / total_weight
        patch_c = patch[:, cols]
        owner = lax.broadcasted_iota(jnp.int32, (VEL, WIDTH), 0) == (patch_c >> 7)
        spread = jnp.where(owner, sens, 0.0)
        piece0 = spread.astype(BF16)
        left = spread - piece0.astype(F32)
        piece1 = left.astype(BF16)
        piece2 = (left - piece1.astype(F32)).astype(BF16)
        slot = lax.broadcasted_iota(jnp.int32, (128, WIDTH), 0) == (patch_c & 15)
        sums = lax.dot_general(
            jnp.concatenate([piece0, piece1, piece2], axis=0),
            jnp.where(slot, 1.0, 0.0).astype(BF16),
            (((1,), (1,)), ((), ())),
            preferred_element_type=F32,
        )
        total[...] += sums[0:VEL] + sums[VEL : 2 * VEL] + sums[2 * VEL :]
        if c == CHUNKS - 1:
            for i in range(VEL):
                part[i] = total[i : i + 1]

            def give(k, _):
                owner = target(k)
                pltpu.make_async_remote_copy(
                    src_ref=part.at[owner], dst_ref=part_in.at[v], send_sem=psend_sem, recv_sem=precv_sem,
                    device_id={"vel": owner}, device_id_type=MESH,
                ).start()
                return 0

            lax.fori_loop(1, VEL, give, 0)

        moments = (fluid * relax_c) * ((first - wall * second) / total_weight)
        high, low = split(moments)
        stacked = jnp.concatenate([high, high, low, low], axis=0)
        keep = fluid * (1.0 - relax_c)
        keep_wall = keep * wall
        for r in range(Q // ROWS):
            rows = pl.ds(r * ROWS, ROWS)
            collided = jnp.dot(btab[rows, 0:64], stacked, preferred_element_type=F32)
            for j in range(WIDTH // 128):
                sub = slice(j * 128, (j + 1) * 128)
                at = pl.ds(c * WIDTH + j * 128, 128)
                factor = keep[:, sub] - keep_wall[:, sub] * absorb_tab[rows, :]
                value = factor * mu[rows, at].astype(F32) + collided[:, sub]
                result[rows, at] = value.astype(BF16)

    part_in[pl.ds(v, 1)] = part[pl.ds(v, 1)]
    sent = part.at[pl.ds(0, VEL - 1)]
    pltpu.make_async_copy(sent, sent, precv_sem).wait()
    grad = part_in[0]
    for i in range(1, VEL):
        grad = grad + part_in[i]
    grad_out[...] = grad

    pltpu.make_async_copy(sent, sent, psend_sem).wait()
    staged_out = staged.at[pl.ds(0, VEL - 1)]
    pltpu.make_async_copy(staged_out, staged_out, send_sem).wait()

    @pl.when(g > 0)
    def _():
        to_lower().wait_send()

    @pl.when(g < GRP - 1)
    def _():
        to_upper().wait_send()


def store_kernel(result, grad, out_hbm, grad_hbm, small, out_sem, grad_sem):
    copies = []
    for c in range(CHUNKS):
        rows = pl.ds(c * (Q // CHUNKS), Q // CHUNKS)
        copies.append(pltpu.make_async_copy(result.at[rows], out_hbm.at[rows], out_sem.at[c]))
    for copy in copies:
        copy.start()
    small[...] = grad[:, 0:PATCH_DEV]
    last = pltpu.make_async_copy(small, grad_hbm, grad_sem)
    last.start()
    for copy in copies:
        copy.wait()
    last.wait()


def in_hbm(x):
    return pltpu.with_memory_space_constraint(x, pltpu.HBM)


def in_vmem(x):
    return pltpu.with_memory_space_constraint(x, pltpu.VMEM)


def body(adjoint, relaxation, reaction, base_moments, cell_kind, patch_id):
    dma = pltpu.SemaphoreType.DMA
    hbm = pl.BlockSpec(memory_space=pltpu.HBM)
    vmem = pl.BlockSpec(memory_space=pltpu.VMEM)
    result, grad = pl.pallas_call(
        kernel,
        out_shape=(pltpu.VMEM((Q, CELLS), BF16), pltpu.VMEM((1, 128), F32)),
        in_specs=[hbm] * 6,
        out_specs=(vmem, vmem),
        scratch_shapes=[
            pltpu.VMEM((LOCAL, XB, CELLS), BF16),
            pltpu.VMEM((XB + 2, LOCAL, CELLS), BF16),
            pltpu.VMEM((XB, LOCAL, CELLS), BF16),
            pltpu.VMEM((Q, CELLS), BF16),
            pltpu.VMEM((1, CELLS), F32),
            pltpu.VMEM((1, CELLS), F32),
            pltpu.VMEM((MOMENTS, 1, CELLS), F32),
            pltpu.VMEM((1, CELLS), jnp.int32),
            pltpu.VMEM((1, CELLS), jnp.int32),
            pltpu.VMEM((Q, 128), F32),
            pltpu.VMEM((64, Q), BF16),
            pltpu.VMEM((Q, 128), BF16),
            pltpu.VMEM((VEL, 1, 128), F32),
            pltpu.VMEM((VEL, 1, 128), F32),
            pltpu.VMEM((VEL, 128), F32),
            dma,
            dma((5,)),
            dma((2,)),
            dma((2,)),
            dma,
            dma((CHUNKS,)),
            dma,
            dma,
        ],
        compiler_params=pltpu.CompilerParams(
            collective_id=0, has_side_effects=True, vmem_limit_bytes=40 * 1024 * 1024
        ),
        name="adjoint_step",
    )(*[in_hbm(x) for x in (adjoint, relaxation, reaction, base_moments, cell_kind, patch_id)])
    out, grad = pl.pallas_call(
        store_kernel,
        out_shape=(jax.ShapeDtypeStruct((Q, CELLS), BF16), jax.ShapeDtypeStruct((1, PATCH_DEV), F32)),
        in_specs=[vmem] * 2,
        out_specs=(hbm, hbm),
        scratch_shapes=[pltpu.VMEM((1, PATCH_DEV), F32), dma((CHUNKS,)), dma],
        compiler_params=pltpu.CompilerParams(vmem_limit_bytes=8 * 1024 * 1024),
        name="store_step",
    )(in_vmem(result), in_vmem(grad))
    return out.reshape(Q, 1, 1, CELLS), grad.reshape(PATCH_DEV)


def solution(mesh):
    placed = (
        P("vel", "grp", None, None),
        P("grp", "vel", None),
        P("grp", "vel", None),
        P(None, "grp", "vel", None),
        P("grp", "vel", None),
        P("grp", "vel", None),
    )
    return jax.shard_map(
        body,
        mesh=mesh,
        in_specs=placed,
        out_specs=(P(None, "grp", "vel", None), P(("vel", "grp"))),
        check_vma=False,
    )
```

```python
import jax
import jax.numpy as jnp
from jax import lax
from jax.experimental import pallas as pl
from jax.experimental.pallas import tpu as pltpu
from jax.sharding import PartitionSpec as P

NV = 8
MOMENTS = 10
PY = 16
PZ = 128
PATCH_DEV = 16
Q = 512
XB = 32
CELLS = PY * PZ
COURANT = 0.3

VEL = 32
GRP = 8
LOCAL = Q // VEL
WIDTHS = (512, 512, 512, 256, 256)
STARTS = tuple(sum(WIDTHS[:i]) for i in range(len(WIDTHS)))
CHUNKS = len(WIDTHS)
EARLY = 2
PIECES = ((0, 640), (1920, 128), (640, 640), (1280, 640))
FIRST = 2
ROWS = 128
STORES = 4
STEP = 13

MESH = pl.DeviceIdType.MESH
F32 = jnp.float32
BF16 = jnp.bfloat16


def component(digit):
    sign = jnp.where((digit & 1) == 0, -1.0, 1.0).astype(F32)
    return sign * ((digit >> 1).astype(F32) + 0.5) / (NV / 2.0 - 0.5)


def velocities(vel_index):
    return (
        component(vel_index & (NV - 1)),
        component((vel_index >> 3) & (NV - 1)),
        component(vel_index >> 6),
    )


def poly(k, ux, uy, uz):
    third = 1.0 / 3.0
    terms = (
        jnp.ones_like(ux),
        ux,
        uy,
        uz,
        ux * ux - third,
        uy * uy - third,
        uz * uz - third,
        ux * uy,
        ux * uz,
        uy * uz,
    )
    value = jnp.zeros_like(ux)
    for i, term in enumerate(terms):
        value = jnp.where(k == i, term, value)
    return value


def split(value):
    high = value.astype(BF16)
    return high, (value - high.astype(F32)).astype(BF16)


def kernel(
    adj_hbm, relax_hbm, react_hbm, base_hbm, kind_hbm, patch_hbm,
    result, grad_out,
    xin, turned, staged, mu, relax, react, base, kind, patch,
    absorb_tab, etab, btab, part, part_in, total,
    load_sem, small_sem, halo_send, halo_recv, send_sem, recv_sem, psend_sem, precv_sem,
):
    v = lax.axis_index("vel")
    g = lax.axis_index("grp")
    core = v & 1

    loads = []
    for i, (start, width) in enumerate(PIECES):
        cols = pl.ds(start, width)
        loads.append(pltpu.make_async_copy(adj_hbm.at[:, 0, :, cols], xin.at[:, :, cols], load_sem.at[i]))
    for copy in loads:
        copy.start()
    smalls = [
        pltpu.make_async_copy(relax_hbm.at[0], relax, small_sem.at[0]),
        pltpu.make_async_copy(react_hbm.at[0], react, small_sem.at[1]),
        pltpu.make_async_copy(kind_hbm.at[0], kind, small_sem.at[2]),
        pltpu.make_async_copy(patch_hbm.at[0], patch, small_sem.at[3]),
        pltpu.make_async_copy(base_hbm.at[:, 0], base, small_sem.at[4]),
    ]
    for copy in smalls:
        copy.start()

    barrier = pltpu.get_barrier_semaphore()

    def greet(k, _):
        pl.semaphore_signal(barrier, inc=1, device_id={"vel": (v + k) & (VEL - 1)}, device_id_type=MESH)
        return 0

    lax.fori_loop(1, VEL, greet, 0)

    @pl.when(g > 0)
    def _():
        pl.semaphore_signal(barrier, inc=1, device_id={"grp": g - 1}, device_id_type=MESH)

    @pl.when(g < GRP - 1)
    def _():
        pl.semaphore_signal(barrier, inc=1, device_id={"grp": g + 1}, device_id_type=MESH)

    row = lax.broadcasted_iota(jnp.int32, (256, 256), 0)
    col = lax.broadcasted_iota(jnp.int32, (256, 256), 1)
    perm = jnp.where(col == ((row & 15) << 4) + (row >> 4), 1.0, 0.0).astype(BF16)

    def turn(i):
        start, width = PIECES[i]
        cols = pl.ds(start, width)
        loads[i].wait()
        for t in range(2):
            block = xin[:, pl.ds(16 * t, 16), cols].reshape(256, width)
            moved = jnp.dot(perm, block, preferred_element_type=F32).astype(BF16)
            turned[pl.ds(1 + 16 * t, 16), :, cols] = moved.reshape(16, LOCAL, width)

    for i in range(FIRST):
        turn(i)

    neighbours = jnp.where(g > 0, 1, 0) + jnp.where(g < GRP - 1, 1, 0)
    pl.semaphore_wait(barrier, VEL - 1 + neighbours)

    def to_lower():
        return pltpu.make_async_remote_copy(
            src_ref=turned.at[1], dst_ref=turned.at[XB + 1], send_sem=halo_send.at[0], recv_sem=halo_recv.at[0],
            device_id={"grp": g - 1}, device_id_type=MESH,
        )

    def to_upper():
        return pltpu.make_async_remote_copy(
            src_ref=turned.at[XB], dst_ref=turned.at[0], send_sem=halo_send.at[1], recv_sem=halo_recv.at[1],
            device_id={"grp": g + 1}, device_id_type=MESH,
        )

    def send_ends():
        @pl.when(g > 0)
        def _():
            to_lower().start()

        @pl.when(g < GRP - 1)
        def _():
            to_upper().start()

        @pl.when(g == 0)
        def _():
            turned[0] = jnp.zeros((LOCAL, CELLS), BF16)

        @pl.when(g == GRP - 1)
        def _():
            turned[XB + 1] = jnp.zeros((LOCAL, CELLS), BF16)

    own = v * LOCAL + lax.broadcasted_iota(jnp.int32, (LOCAL, PZ), 0)
    ux, uy, uz = velocities(own)
    rate_x, rate_y, rate_z = COURANT * jnp.abs(ux), COURANT * jnp.abs(uy), COURANT * jnp.abs(uz)
    rest = 1.0 - rate_x - rate_y - rate_z
    forward_x = ux > 0
    half = LOCAL // 2
    shift_z = jnp.where(((v >> 2) & 1) == 1, PZ - 1, 1)

    def advect(layer, c, store):
        count = WIDTHS[c] // PZ
        base_block = STARTS[c] // PZ

        def cells(at, j):
            return turned[at, :, pl.ds((j % PY) * PZ, PZ)].astype(F32)

        centre = [cells(layer + 1, base_block + j) for j in range(-1, count + 1)]
        for j in range(count):
            block = centre[j + 1]
            along_x = jnp.where(forward_x, cells(layer + 2, base_block + j), cells(layer, base_block + j))
            along_y = jnp.concatenate([centre[j][:half], centre[j + 2][half:]], axis=0)
            along_z = pltpu.roll(block, shift_z, 1)
            value = rest * block + rate_x * along_x + rate_y * along_y + rate_z * along_z
            store(pl.ds((base_block + j) * PZ, PZ), value.astype(BF16))

    def target(k):
        o = (k * STEP) & (VEL - 1)
        da, db, dc = (o >> 1) & 3, o >> 3, o & 1
        dx = jnp.where(core == 0, da, db)
        dy = jnp.where(core == 0, db, da)
        y, x = v >> 3, (v >> 1) & 3
        return (((y + dy) & 3) << 3) + (((x + dx) & 3) << 1) + ((core + dc) & 1)

    own_rows = pl.ds(pl.multiple_of(v * LOCAL, LOCAL), LOCAL)

    def advect_and_send(layer, c):
        cols = pl.ds(STARTS[c], WIDTHS[c])

        def store(at, value):
            staged[layer, :, at] = value

        advect(layer, c, store)
        pltpu.make_async_remote_copy(
            src_ref=staged.at[layer, :, cols], dst_ref=mu.at[own_rows, cols], send_sem=send_sem, recv_sem=recv_sem.at[c],
            device_id={"vel": layer}, device_id_type=MESH,
        ).start()

    for c in range(CHUNKS):

        def step(k, _):
            layer = target(k)
            if c < EARLY:

                @pl.when((layer > 0) & (layer < XB - 1))
                def _():
                    advect_and_send(layer, c)
            else:
                advect_and_send(layer, c)
            return 0

        lax.fori_loop(1, VEL, step, 0)
        if c == 0:
            for i in range(FIRST, len(PIECES)):
                turn(i)
            send_ends()
        if c == EARLY - 1:

            @pl.when(g > 0)
            def _():
                to_upper().wait_recv()

            @pl.when(g < GRP - 1)
            def _():
                to_lower().wait_recv()

            for layer in (0, XB - 1):

                @pl.when(v != layer)
                def _():
                    for early in range(EARLY):
                        advect_and_send(layer, early)

    def store_own(at, value):
        mu[own_rows, at] = value

    for c in range(CHUNKS):
        advect(v, c, store_own)

    q_row = lax.broadcasted_iota(jnp.int32, (64, Q), 1)
    j_row = lax.broadcasted_iota(jnp.int32, (64, Q), 0)
    ux, uy, uz = velocities(q_row)
    speed = ux * ux + uy * uy + uz * uz
    weight = jnp.exp(-speed)
    total_weight = jnp.sum(weight[0:8], axis=1, keepdims=True)[0:1]
    entry = poly(j_row & 15, ux, uy, uz) * jnp.where((j_row & 16) == 0, weight, weight * (speed / 3.0))
    high = entry.astype(BF16).astype(F32)
    etab[...] = jnp.where(j_row < 32, high, entry - high).astype(BF16)

    for r in range(Q // ROWS):
        rows = pl.ds(r * ROWS, ROWS)
        q_col = r * ROWS + lax.broadcasted_iota(jnp.int32, (ROWS, 128), 0)
        j_col = lax.broadcasted_iota(jnp.int32, (ROWS, 128), 1)
        ux, uy, uz = velocities(q_col)
        absorb_tab[rows, :] = (ux * ux + uy * uy + uz * uz) / 3.0
        entry = poly(j_col & 15, ux, uy, uz)
        high = entry.astype(BF16).astype(F32)
        btab[rows, :] = jnp.where((j_col & 16) == 0, high, entry - high).astype(BF16)

    for copy in smalls:
        copy.wait()

    total[...] = jnp.zeros((VEL, 128), F32)
    for c in range(CHUNKS):
        cols = pl.ds(STARTS[c], WIDTHS[c])
        arrived = mu.at[pl.ds(0, (VEL - 1) * LOCAL), cols]
        pltpu.make_async_copy(arrived, arrived, recv_sem.at[c]).wait()
        product = jnp.dot(etab[...], mu[:, cols], preferred_element_type=F32)
        first = product[0:16] + product[32:48]
        second = product[16:32] + product[48:64]
        kind_c = kind[:, cols]
        wall = jnp.where(kind_c == 2, react[:, cols], 0.0)
        fluid = jnp.where(kind_c != 0, 1.0, 0.0)
        relax_c = relax[:, cols]

        acc = base[0, :, cols] * second[0:1]
        for k in range(1, MOMENTS):
            acc = acc + base[k, :, cols] * second[k : k + 1]
        sens = -wall * acc / total_weight
        patch_c = patch[:, cols]
        owner = lax.broadcasted_iota(jnp.int32, (VEL, WIDTHS[c]), 0) == (patch_c >> 7)
        spread = jnp.where(owner, sens, 0.0)
        piece0 = spread.astype(BF16)
        left = spread - piece0.astype(F32)
        piece1 = left.astype(BF16)
        piece2 = (left - piece1.astype(F32)).astype(BF16)
        slot = lax.broadcasted_iota(jnp.int32, (128, WIDTHS[c]), 0) == (patch_c & 15)
        sums = lax.dot_general(
            jnp.concatenate([piece0, piece1, piece2], axis=0),
            jnp.where(slot, 1.0, 0.0).astype(BF16),
            (((1,), (1,)), ((), ())),
            preferred_element_type=F32,
        )
        total[...] += sums[0:VEL] + sums[VEL : 2 * VEL] + sums[2 * VEL :]
        if c == CHUNKS - 1:
            for i in range(VEL):
                part[i] = total[i : i + 1]

            def give(k, _):
                owner = target(k)
                pltpu.make_async_remote_copy(
                    src_ref=part.at[owner], dst_ref=part_in.at[v], send_sem=psend_sem, recv_sem=precv_sem,
                    device_id={"vel": owner}, device_id_type=MESH,
                ).start()
                return 0

            lax.fori_loop(1, VEL, give, 0)

        moments = (fluid * relax_c) * ((first - wall * second) / total_weight)
        high, low = split(moments)
        stacked = jnp.concatenate([high, high, low, low], axis=0)
        keep = fluid * (1.0 - relax_c)
        keep_wall = keep * wall
        for r in range(Q // ROWS):
            rows = pl.ds(r * ROWS, ROWS)
            collided = jnp.dot(btab[rows, 0:64], stacked, preferred_element_type=F32)
            for j in range(WIDTHS[c] // 128):
                sub = slice(j * 128, (j + 1) * 128)
                at = pl.ds(STARTS[c] + j * 128, 128)
                factor = keep[:, sub] - keep_wall[:, sub] * absorb_tab[rows, :]
                value = factor * mu[rows, at].astype(F32) + collided[:, sub]
                result[rows, at] = value.astype(BF16)

    part_in[pl.ds(v, 1)] = part[pl.ds(v, 1)]
    sent = part.at[pl.ds(0, VEL - 1)]
    pltpu.make_async_copy(sent, sent, precv_sem).wait()
    grad = part_in[0]
    for i in range(1, VEL):
        grad = grad + part_in[i]
    grad_out[...] = grad

    pltpu.make_async_copy(sent, sent, psend_sem).wait()
    staged_out = staged.at[pl.ds(0, VEL - 1)]
    pltpu.make_async_copy(staged_out, staged_out, send_sem).wait()

    @pl.when(g > 0)
    def _():
        to_lower().wait_send()

    @pl.when(g < GRP - 1)
    def _():
        to_upper().wait_send()


def store_kernel(result, grad, out_hbm, grad_hbm, small, out_sem, grad_sem):
    copies = []
    for c in range(STORES):
        rows = pl.ds(c * (Q // STORES), Q // STORES)
        copies.append(pltpu.make_async_copy(result.at[rows], out_hbm.at[rows], out_sem.at[c]))
    for copy in copies:
        copy.start()
    small[...] = grad[:, 0:PATCH_DEV]
    last = pltpu.make_async_copy(small, grad_hbm, grad_sem)
    last.start()
    for copy in copies:
        copy.wait()
    last.wait()


def in_hbm(x):
    return pltpu.with_memory_space_constraint(x, pltpu.HBM)


def in_vmem(x):
    return pltpu.with_memory_space_constraint(x, pltpu.VMEM)


def body(adjoint, relaxation, reaction, base_moments, cell_kind, patch_id):
    dma = pltpu.SemaphoreType.DMA
    hbm = pl.BlockSpec(memory_space=pltpu.HBM)
    vmem = pl.BlockSpec(memory_space=pltpu.VMEM)
    result, grad = pl.pallas_call(
        kernel,
        out_shape=(pltpu.VMEM((Q, CELLS), BF16), pltpu.VMEM((1, 128), F32)),
        in_specs=[hbm] * 6,
        out_specs=(vmem, vmem),
        scratch_shapes=[
            pltpu.VMEM((LOCAL, XB, CELLS), BF16),
            pltpu.VMEM((XB + 2, LOCAL, CELLS), BF16),
            pltpu.VMEM((XB, LOCAL, CELLS), BF16),
            pltpu.VMEM((Q, CELLS), BF16),
            pltpu.VMEM((1, CELLS), F32),
            pltpu.VMEM((1, CELLS), F32),
            pltpu.VMEM((MOMENTS, 1, CELLS), F32),
            pltpu.VMEM((1, CELLS), jnp.int32),
            pltpu.VMEM((1, CELLS), jnp.int32),
            pltpu.VMEM((Q, 128), F32),
            pltpu.VMEM((64, Q), BF16),
            pltpu.VMEM((Q, 128), BF16),
            pltpu.VMEM((VEL, 1, 128), F32),
            pltpu.VMEM((VEL, 1, 128), F32),
            pltpu.VMEM((VEL, 128), F32),
            dma((len(PIECES),)),
            dma((5,)),
            dma((2,)),
            dma((2,)),
            dma,
            dma((CHUNKS,)),
            dma,
            dma,
        ],
        compiler_params=pltpu.CompilerParams(
            collective_id=0, has_side_effects=True, vmem_limit_bytes=40 * 1024 * 1024
        ),
        name="adjoint_step",
    )(*[in_hbm(x) for x in (adjoint, relaxation, reaction, base_moments, cell_kind, patch_id)])
    out, grad = pl.pallas_call(
        store_kernel,
        out_shape=(jax.ShapeDtypeStruct((Q, CELLS), BF16), jax.ShapeDtypeStruct((1, PATCH_DEV), F32)),
        in_specs=[vmem] * 2,
        out_specs=(hbm, hbm),
        scratch_shapes=[pltpu.VMEM((1, PATCH_DEV), F32), dma((STORES,)), dma],
        compiler_params=pltpu.CompilerParams(vmem_limit_bytes=8 * 1024 * 1024),
        name="store_step",
    )(in_vmem(result), in_vmem(grad))
    return out.reshape(Q, 1, 1, CELLS), grad.reshape(PATCH_DEV)


def solution(mesh):
    placed = (
        P("vel", "grp", None, None),
        P("grp", "vel", None),
        P("grp", "vel", None),
        P(None, "grp", "vel", None),
        P("grp", "vel", None),
        P("grp", "vel", None),
    )
    return jax.shard_map(
        body,
        mesh=mesh,
        in_specs=placed,
        out_specs=(P(None, "grp", "vel", None), P(("vel", "grp"))),
        check_vma=False,
    )
```

```python
import jax
import jax.numpy as jnp
from jax import lax
from jax.experimental import pallas as pl
from jax.experimental.pallas import tpu as pltpu
from jax.sharding import PartitionSpec as P

NV = 8
MOMENTS = 10
PY = 16
PZ = 128
PATCH_DEV = 16
Q = 512
XB = 32
CELLS = PY * PZ
COURANT = 0.3

VEL = 32
GRP = 8
LOCAL = Q // VEL
WIDTHS = (512, 512, 512, 512)
STARTS = tuple(sum(WIDTHS[:i]) for i in range(len(WIDTHS)))
CHUNKS = len(WIDTHS)
PIECES = ((0, 512), (512, 512), (1024, 512), (1536, 512))
CHIPS = (1, 4, 3, 12, 5, 15, 2, 8, 13, 7, 6, 9, 14, 11, 10)
ONE, TWO, THREE, FOUR = (0, 4), (4, 10), (10, 14), (14, 15)
PACKED = tuple(sum(chip << (4 * i) for i, chip in enumerate(CHIPS[at : at + 7])) for at in (0, 7, 14))
ROWS = 128
STORES = 4

MESH = pl.DeviceIdType.MESH
F32 = jnp.float32
BF16 = jnp.bfloat16


def component(digit):
    sign = jnp.where((digit & 1) == 0, -1.0, 1.0).astype(F32)
    return sign * ((digit >> 1).astype(F32) + 0.5) / (NV / 2.0 - 0.5)


def velocities(vel_index):
    return (
        component(vel_index & (NV - 1)),
        component((vel_index >> 3) & (NV - 1)),
        component(vel_index >> 6),
    )


def poly(k, ux, uy, uz):
    third = 1.0 / 3.0
    terms = (
        jnp.ones_like(ux),
        ux,
        uy,
        uz,
        ux * ux - third,
        uy * uy - third,
        uz * uz - third,
        ux * uy,
        ux * uz,
        uy * uz,
    )
    value = jnp.zeros_like(ux)
    for i, term in enumerate(terms):
        value = jnp.where(k == i, term, value)
    return value


def split(value):
    high = value.astype(BF16)
    return high, (value - high.astype(F32)).astype(BF16)


def kernel(
    adj_hbm, relax_hbm, react_hbm, base_hbm, kind_hbm, patch_hbm,
    result, grad_out,
    xin, turned, staged, mu, relax, react, base, kind, patch,
    absorb_tab, etab, btab, part, part_in, total,
    round_sem, load_sem, small_sem, halo_send, halo_recv, send_sem, recv_sem, psend_sem, precv_sem,
):
    v = lax.axis_index("vel")
    g = lax.axis_index("grp")
    core = v & 1

    loads = []
    for i, (start, width) in enumerate(PIECES):
        cols = pl.ds(start, width)
        loads.append(pltpu.make_async_copy(adj_hbm.at[:, 0, :, cols], xin.at[:, :, cols], load_sem.at[i]))
    for copy in loads:
        copy.start()
    smalls = [
        pltpu.make_async_copy(relax_hbm.at[0], relax, small_sem.at[0]),
        pltpu.make_async_copy(react_hbm.at[0], react, small_sem.at[1]),
        pltpu.make_async_copy(kind_hbm.at[0], kind, small_sem.at[2]),
        pltpu.make_async_copy(patch_hbm.at[0], patch, small_sem.at[3]),
        pltpu.make_async_copy(base_hbm.at[:, 0], base, small_sem.at[4]),
    ]
    for copy in smalls:
        copy.start()

    def device(dx, dy, dc):
        y, x = v >> 3, (v >> 1) & 3
        return (((y + dy) & 3) << 3) + (((x + dx) & 3) << 1) + ((core + dc) & 1)

    barrier = pltpu.get_barrier_semaphore()
    hops = ((1, 0), (0, 1), (3, 0), (0, 3))
    nearest = [(0, 0, 1)] + [(dx, dy, dc) for dx, dy in hops for dc in (0, 1)]
    for at in nearest:
        pl.semaphore_signal(barrier, inc=1, device_id={"vel": device(*at)}, device_id_type=MESH)

    @pl.when(g > 0)
    def _():
        pl.semaphore_signal(barrier, inc=1, device_id={"grp": g - 1}, device_id_type=MESH)

    @pl.when(g < GRP - 1)
    def _():
        pl.semaphore_signal(barrier, inc=1, device_id={"grp": g + 1}, device_id_type=MESH)

    def tell(i):
        for dx, dy in hops:
            pl.semaphore_signal(round_sem.at[i], inc=1, device_id={"vel": device(dx, dy, 0)}, device_id_type=MESH)

    def hear(i):
        pl.semaphore_wait(round_sem.at[i], len(hops))

    row = lax.broadcasted_iota(jnp.int32, (256, 256), 0)
    col = lax.broadcasted_iota(jnp.int32, (256, 256), 1)
    perm = jnp.where(col == ((row & 15) << 4) + (row >> 4), 1.0, 0.0).astype(BF16)

    def turn(i):
        start, width = PIECES[i]
        cols = pl.ds(start, width)
        loads[i].wait()
        for t in range(2):
            block = xin[:, pl.ds(16 * t, 16), cols].reshape(256, width)
            moved = jnp.dot(perm, block, preferred_element_type=F32).astype(BF16)
            turned[pl.ds(1 + 16 * t, 16), :, cols] = moved.reshape(16, LOCAL, width)

    for i in range(len(PIECES)):
        turn(i)

    neighbours = jnp.where(g > 0, 1, 0) + jnp.where(g < GRP - 1, 1, 0)
    pl.semaphore_wait(barrier, len(nearest) + neighbours)
    tell(0)

    def to_lower():
        return pltpu.make_async_remote_copy(
            src_ref=turned.at[1], dst_ref=turned.at[XB + 1], send_sem=halo_send.at[0], recv_sem=halo_recv.at[0],
            device_id={"grp": g - 1}, device_id_type=MESH,
        )

    def to_upper():
        return pltpu.make_async_remote_copy(
            src_ref=turned.at[XB], dst_ref=turned.at[0], send_sem=halo_send.at[1], recv_sem=halo_recv.at[1],
            device_id={"grp": g + 1}, device_id_type=MESH,
        )

    @pl.when(g > 0)
    def _():
        to_lower().start()

    @pl.when(g < GRP - 1)
    def _():
        to_upper().start()

    @pl.when(g == 0)
    def _():
        turned[0] = jnp.zeros((LOCAL, CELLS), BF16)

    @pl.when(g == GRP - 1)
    def _():
        turned[XB + 1] = jnp.zeros((LOCAL, CELLS), BF16)

    own = v * LOCAL + lax.broadcasted_iota(jnp.int32, (LOCAL, PZ), 0)
    ux, uy, uz = velocities(own)
    rate_x, rate_y, rate_z = COURANT * jnp.abs(ux), COURANT * jnp.abs(uy), COURANT * jnp.abs(uz)
    rest = 1.0 - rate_x - rate_y - rate_z
    forward_x = ux > 0
    half = LOCAL // 2
    shift_z = jnp.where(((v >> 2) & 1) == 1, PZ - 1, 1)

    def advect(layer, c, store):
        count = WIDTHS[c] // PZ
        base_block = STARTS[c] // PZ

        def cells(at, j):
            return turned[at, :, pl.ds((j % PY) * PZ, PZ)].astype(F32)

        centre = [cells(layer + 1, base_block + j) for j in range(-1, count + 1)]
        for j in range(count):
            block = centre[j + 1]
            along_x = jnp.where(forward_x, cells(layer + 2, base_block + j), cells(layer, base_block + j))
            along_y = jnp.concatenate([centre[j][:half], centre[j + 2][half:]], axis=0)
            along_z = pltpu.roll(block, shift_z, 1)
            value = rest * block + rate_x * along_x + rate_y * along_y + rate_z * along_z
            store(pl.ds((base_block + j) * PZ, PZ), value.astype(BF16))

    def chip(k):
        word = jnp.where(k < 7, PACKED[0], jnp.where(k < 14, PACKED[1], PACKED[2]))
        code = (word >> (4 * lax.rem(k, 7))) & 15
        da, db = code & 3, code >> 2
        return jnp.where(core == 0, da, db), jnp.where(core == 0, db, da)

    own_rows = pl.ds(pl.multiple_of(v * LOCAL, LOCAL), LOCAL)

    def advect_and_send(layer, c):
        cols = pl.ds(STARTS[c], WIDTHS[c])

        def store(at, value):
            staged[layer, :, at] = value

        advect(layer, c, store)
        pltpu.make_async_remote_copy(
            src_ref=staged.at[layer, :, cols], dst_ref=mu.at[own_rows, cols], send_sem=send_sem, recv_sem=recv_sem.at[c],
            device_id={"vel": layer}, device_id_type=MESH,
        ).start()

    def to_sibling(c, inner):
        layer = v ^ 1
        if inner:

            @pl.when((layer > 0) & (layer < XB - 1))
            def _():
                advect_and_send(layer, c)
        else:
            advect_and_send(layer, c)

    def to_chips(span, c, inner=False, back=False):
        def step(i, _):
            dx, dy = chip(span[0] + span[1] - 1 - i if back else i)
            for dc in (0, 1):
                layer = device(dx, dy, dc)
                if inner:

                    @pl.when((layer > 0) & (layer < XB - 1))
                    def _():
                        advect_and_send(layer, c)
                else:
                    advect_and_send(layer, c)
            return 0

        lax.fori_loop(span[0], span[1], step, 0)

    ahead = 3
    for c in range(ahead):
        to_sibling(c, True)
        to_chips(ONE, c, True)
    hear(0)
    tell(1)

    @pl.when(g > 0)
    def _():
        to_upper().wait_recv()

    @pl.when(g < GRP - 1)
    def _():
        to_lower().wait_recv()

    for layer in (0, XB - 1):
        far_x = ((v >> 1) - (layer >> 1)) & 3
        far_y = ((v >> 3) - (layer >> 3)) & 3
        far = jnp.minimum(far_x, 4 - far_x) + jnp.minimum(far_y, 4 - far_y)

        @pl.when((far <= 1) & (v != layer))
        def _():
            for c in range(ahead):
                advect_and_send(layer, c)

    to_chips(TWO, 0)
    hear(1)
    tell(2)
    to_chips(TWO, 1)
    to_chips(THREE, 0)
    hear(2)
    to_chips(FOUR, 0)
    to_chips((THREE[0], FOUR[1]), 1)
    to_chips((TWO[0], FOUR[1]), 2)
    to_chips((ONE[0], FOUR[1]), 3, back=True)
    to_sibling(3, False)

    def store_own(at, value):
        mu[own_rows, at] = value

    for c in range(CHUNKS):
        advect(v, c, store_own)

    q_row = lax.broadcasted_iota(jnp.int32, (64, Q), 1)
    j_row = lax.broadcasted_iota(jnp.int32, (64, Q), 0)
    ux, uy, uz = velocities(q_row)
    speed = ux * ux + uy * uy + uz * uz
    weight = jnp.exp(-speed)
    total_weight = jnp.sum(weight[0:8], axis=1, keepdims=True)[0:1]
    entry = poly(j_row & 15, ux, uy, uz) * jnp.where((j_row & 16) == 0, weight, weight * (speed / 3.0))
    high = entry.astype(BF16).astype(F32)
    etab[...] = jnp.where(j_row < 32, high, entry - high).astype(BF16)

    for r in range(Q // ROWS):
        rows = pl.ds(r * ROWS, ROWS)
        q_col = r * ROWS + lax.broadcasted_iota(jnp.int32, (ROWS, 128), 0)
        j_col = lax.broadcasted_iota(jnp.int32, (ROWS, 128), 1)
        ux, uy, uz = velocities(q_col)
        absorb_tab[rows, :] = (ux * ux + uy * uy + uz * uz) / 3.0
        entry = poly(j_col & 15, ux, uy, uz)
        high = entry.astype(BF16).astype(F32)
        btab[rows, :] = jnp.where((j_col & 16) == 0, high, entry - high).astype(BF16)

    for copy in smalls:
        copy.wait()

    total[...] = jnp.zeros((VEL, 128), F32)
    for c in range(CHUNKS):
        cols = pl.ds(STARTS[c], WIDTHS[c])
        arrived = mu.at[pl.ds(0, (VEL - 1) * LOCAL), cols]
        pltpu.make_async_copy(arrived, arrived, recv_sem.at[c]).wait()
        product = jnp.dot(etab[...], mu[:, cols], preferred_element_type=F32)
        first = product[0:16] + product[32:48]
        second = product[16:32] + product[48:64]
        kind_c = kind[:, cols]
        wall = jnp.where(kind_c == 2, react[:, cols], 0.0)
        fluid = jnp.where(kind_c != 0, 1.0, 0.0)
        relax_c = relax[:, cols]

        acc = base[0, :, cols] * second[0:1]
        for k in range(1, MOMENTS):
            acc = acc + base[k, :, cols] * second[k : k + 1]
        sens = -wall * acc / total_weight
        patch_c = patch[:, cols]
        owner = lax.broadcasted_iota(jnp.int32, (VEL, WIDTHS[c]), 0) == (patch_c >> 7)
        spread = jnp.where(owner, sens, 0.0)
        piece0 = spread.astype(BF16)
        left = spread - piece0.astype(F32)
        piece1 = left.astype(BF16)
        piece2 = (left - piece1.astype(F32)).astype(BF16)
        slot = lax.broadcasted_iota(jnp.int32, (128, WIDTHS[c]), 0) == (patch_c & 15)
        sums = lax.dot_general(
            jnp.concatenate([piece0, piece1, piece2], axis=0),
            jnp.where(slot, 1.0, 0.0).astype(BF16),
            (((1,), (1,)), ((), ())),
            preferred_element_type=F32,
        )
        total[...] += sums[0:VEL] + sums[VEL : 2 * VEL] + sums[2 * VEL :]
        if c == CHUNKS - 1:
            for i in range(VEL):
                part[i] = total[i : i + 1]

            def give(owner):
                pltpu.make_async_remote_copy(
                    src_ref=part.at[owner], dst_ref=part_in.at[v], send_sem=psend_sem, recv_sem=precv_sem,
                    device_id={"vel": owner}, device_id_type=MESH,
                ).start()

            def give_chip(i, _):
                dx, dy = chip(len(CHIPS) - 1 - i)
                for dc in (0, 1):
                    give(device(dx, dy, dc))
                return 0

            lax.fori_loop(0, len(CHIPS), give_chip, 0)
            give(v ^ 1)

        moments = (fluid * relax_c) * ((first - wall * second) / total_weight)
        high, low = split(moments)
        stacked = jnp.concatenate([high, high, low, low], axis=0)
        keep = fluid * (1.0 - relax_c)
        keep_wall = keep * wall
        for r in range(Q // ROWS):
            rows = pl.ds(r * ROWS, ROWS)
            collided = jnp.dot(btab[rows, 0:64], stacked, preferred_element_type=F32)
            for j in range(WIDTHS[c] // 128):
                sub = slice(j * 128, (j + 1) * 128)
                at = pl.ds(STARTS[c] + j * 128, 128)
                factor = keep[:, sub] - keep_wall[:, sub] * absorb_tab[rows, :]
                value = factor * mu[rows, at].astype(F32) + collided[:, sub]
                result[rows, at] = value.astype(BF16)

    part_in[pl.ds(v, 1)] = part[pl.ds(v, 1)]
    sent = part.at[pl.ds(0, VEL - 1)]
    pltpu.make_async_copy(sent, sent, precv_sem).wait()
    grad = part_in[0]
    for i in range(1, VEL):
        grad = grad + part_in[i]
    grad_out[...] = grad

    pltpu.make_async_copy(sent, sent, psend_sem).wait()
    staged_out = staged.at[pl.ds(0, VEL - 1)]
    pltpu.make_async_copy(staged_out, staged_out, send_sem).wait()

    @pl.when(g > 0)
    def _():
        to_lower().wait_send()

    @pl.when(g < GRP - 1)
    def _():
        to_upper().wait_send()


def store_kernel(result, grad, out_hbm, grad_hbm, small, out_sem, grad_sem):
    copies = []
    for c in range(STORES):
        rows = pl.ds(c * (Q // STORES), Q // STORES)
        copies.append(pltpu.make_async_copy(result.at[rows], out_hbm.at[rows], out_sem.at[c]))
    for copy in copies:
        copy.start()
    small[...] = grad[:, 0:PATCH_DEV]
    last = pltpu.make_async_copy(small, grad_hbm, grad_sem)
    last.start()
    for copy in copies:
        copy.wait()
    last.wait()


def in_hbm(x):
    return pltpu.with_memory_space_constraint(x, pltpu.HBM)


def in_vmem(x):
    return pltpu.with_memory_space_constraint(x, pltpu.VMEM)


def body(adjoint, relaxation, reaction, base_moments, cell_kind, patch_id):
    dma = pltpu.SemaphoreType.DMA
    hbm = pl.BlockSpec(memory_space=pltpu.HBM)
    vmem = pl.BlockSpec(memory_space=pltpu.VMEM)
    result, grad = pl.pallas_call(
        kernel,
        out_shape=(pltpu.VMEM((Q, CELLS), BF16), pltpu.VMEM((1, 128), F32)),
        in_specs=[hbm] * 6,
        out_specs=(vmem, vmem),
        scratch_shapes=[
            pltpu.VMEM((LOCAL, XB, CELLS), BF16),
            pltpu.VMEM((XB + 2, LOCAL, CELLS), BF16),
            pltpu.VMEM((XB, LOCAL, CELLS), BF16),
            pltpu.VMEM((Q, CELLS), BF16),
            pltpu.VMEM((1, CELLS), F32),
            pltpu.VMEM((1, CELLS), F32),
            pltpu.VMEM((MOMENTS, 1, CELLS), F32),
            pltpu.VMEM((1, CELLS), jnp.int32),
            pltpu.VMEM((1, CELLS), jnp.int32),
            pltpu.VMEM((Q, 128), F32),
            pltpu.VMEM((64, Q), BF16),
            pltpu.VMEM((Q, 128), BF16),
            pltpu.VMEM((VEL, 1, 128), F32),
            pltpu.VMEM((VEL, 1, 128), F32),
            pltpu.VMEM((VEL, 128), F32),
            pltpu.SemaphoreType.REGULAR((3,)),
            dma((len(PIECES),)),
            dma((5,)),
            dma((2,)),
            dma((2,)),
            dma,
            dma((CHUNKS,)),
            dma,
            dma,
        ],
        compiler_params=pltpu.CompilerParams(
            collective_id=0, has_side_effects=True, vmem_limit_bytes=40 * 1024 * 1024
        ),
        name="adjoint_step",
    )(*[in_hbm(x) for x in (adjoint, relaxation, reaction, base_moments, cell_kind, patch_id)])
    out, grad = pl.pallas_call(
        store_kernel,
        out_shape=(jax.ShapeDtypeStruct((Q, CELLS), BF16), jax.ShapeDtypeStruct((1, PATCH_DEV), F32)),
        in_specs=[vmem] * 2,
        out_specs=(hbm, hbm),
        scratch_shapes=[pltpu.VMEM((1, PATCH_DEV), F32), dma((STORES,)), dma],
        compiler_params=pltpu.CompilerParams(vmem_limit_bytes=8 * 1024 * 1024),
        name="store_step",
    )(in_vmem(result), in_vmem(grad))
    return out.reshape(Q, 1, 1, CELLS), grad.reshape(PATCH_DEV)


def solution(mesh):
    placed = (
        P("vel", "grp", None, None),
        P("grp", "vel", None),
        P("grp", "vel", None),
        P(None, "grp", "vel", None),
        P("grp", "vel", None),
        P("grp", "vel", None),
    )
    return jax.shard_map(
        body,
        mesh=mesh,
        in_specs=placed,
        out_specs=(P(None, "grp", "vel", None), P(("vel", "grp"))),
        check_vma=False,
    )
```

```python
import jax
import jax.numpy as jnp
from jax import lax
from jax.experimental import pallas as pl
from jax.experimental.pallas import tpu as pltpu
from jax.sharding import PartitionSpec as P

NV = 8
MOMENTS = 10
PY = 16
PZ = 128
PATCH_DEV = 16
Q = 512
XB = 32
CELLS = PY * PZ
COURANT = 0.3

VEL = 32
GRP = 8
LOCAL = Q // VEL
CHUNKS = 4
WIDTH = CELLS // CHUNKS
BLOCKS = WIDTH // PZ
PAIRS = ((6, 14), (9, 11), (5, 15), (13, 7), (2, 8), (1, 3), (4, 12))
FARTHEST = 10
PACKED = tuple(sum(pair[member] << (4 * i) for i, pair in enumerate(PAIRS)) for member in (0, 1))
ROWS = 128
TABLE = 32
STORES = 4

MESH = pl.DeviceIdType.MESH
F32 = jnp.float32
BF16 = jnp.bfloat16


def component(digit):
    sign = jnp.where((digit & 1) == 0, -1.0, 1.0).astype(F32)
    return sign * ((digit >> 1).astype(F32) + 0.5) / (NV / 2.0 - 0.5)


def velocities(vel_index):
    return (
        component(vel_index & (NV - 1)),
        component((vel_index >> 3) & (NV - 1)),
        component(vel_index >> 6),
    )


def poly(k, ux, uy, uz):
    third = 1.0 / 3.0
    terms = (
        jnp.ones_like(ux),
        ux,
        uy,
        uz,
        ux * ux - third,
        uy * uy - third,
        uz * uz - third,
        ux * uy,
        ux * uz,
        uy * uz,
    )
    value = jnp.zeros_like(ux)
    for i, term in enumerate(terms):
        value = jnp.where(k == i, term, value)
    return value


def split(value):
    high = value.astype(BF16)
    return high, (value - high.astype(F32)).astype(BF16)


def kernel(
    adj_hbm, relax_hbm, react_hbm, base_hbm, kind_hbm, patch_hbm,
    result, grad_out,
    xin, turned, staged, mu, relax, react, base, kind, patch,
    absorb_tab, etab, btab, part, part_in, total,
    load_sem, small_sem, halo_send, halo_recv, send_sem, recv_sem, psend_sem, precv_sem,
):
    v = lax.axis_index("vel")
    g = lax.axis_index("grp")
    core = v & 1

    def chunk(c):
        return pl.ds(c * WIDTH, WIDTH) if isinstance(c, int) else pl.ds(pl.multiple_of(c * WIDTH, WIDTH), WIDTH)

    def load(i):
        return pltpu.make_async_copy(adj_hbm.at[:, 0, :, chunk(i)], xin.at[:, :, chunk(i)], load_sem.at[i])

    for i in range(CHUNKS):
        load(i).start()
    smalls = [
        pltpu.make_async_copy(relax_hbm.at[0], relax, small_sem.at[0]),
        pltpu.make_async_copy(react_hbm.at[0], react, small_sem.at[1]),
        pltpu.make_async_copy(kind_hbm.at[0], kind, small_sem.at[2]),
        pltpu.make_async_copy(patch_hbm.at[0], patch, small_sem.at[3]),
        pltpu.make_async_copy(base_hbm.at[:, 0], base, small_sem.at[4]),
    ]
    for copy in smalls:
        copy.start()

    def device(dx, dy, dc):
        y, x = v >> 3, (v >> 1) & 3
        return (((y + dy) & 3) << 3) + (((x + dx) & 3) << 1) + ((core + dc) & 1)

    barrier = pltpu.get_barrier_semaphore()

    def greet(k, _):
        pl.semaphore_signal(barrier, inc=1, device_id={"vel": (v + k) & (VEL - 1)}, device_id_type=MESH)
        return 0

    lax.fori_loop(1, VEL, greet, 0)

    @pl.when(g > 0)
    def _():
        pl.semaphore_signal(barrier, inc=1, device_id={"grp": g - 1}, device_id_type=MESH)

    @pl.when(g < GRP - 1)
    def _():
        pl.semaphore_signal(barrier, inc=1, device_id={"grp": g + 1}, device_id_type=MESH)

    for i in range(CHUNKS):
        load(i).wait()
        for t in range(XB // 16):
            block = xin[:, pl.ds(16 * t, 16), chunk(i)]
            turned[pl.ds(1 + 16 * t, 16), :, chunk(i)] = jnp.swapaxes(block, 0, 1)

    neighbours = jnp.where(g > 0, 1, 0) + jnp.where(g < GRP - 1, 1, 0)
    pl.semaphore_wait(barrier, VEL - 1 + neighbours)

    def to_lower():
        return pltpu.make_async_remote_copy(
            src_ref=turned.at[1], dst_ref=turned.at[XB + 1], send_sem=halo_send.at[0], recv_sem=halo_recv.at[0],
            device_id={"grp": g - 1}, device_id_type=MESH,
        )

    def to_upper():
        return pltpu.make_async_remote_copy(
            src_ref=turned.at[XB], dst_ref=turned.at[0], send_sem=halo_send.at[1], recv_sem=halo_recv.at[1],
            device_id={"grp": g + 1}, device_id_type=MESH,
        )

    @pl.when(g > 0)
    def _():
        to_lower().start()

    @pl.when(g < GRP - 1)
    def _():
        to_upper().start()

    @pl.when(g == 0)
    def _():
        turned[0] = jnp.zeros((LOCAL, CELLS), BF16)

    @pl.when(g == GRP - 1)
    def _():
        turned[XB + 1] = jnp.zeros((LOCAL, CELLS), BF16)

    own = v * LOCAL + lax.broadcasted_iota(jnp.int32, (LOCAL, PZ), 0)
    ux, uy, uz = velocities(own)
    rate_x, rate_y, rate_z = COURANT * jnp.abs(ux), COURANT * jnp.abs(uy), COURANT * jnp.abs(uz)
    rest = 1.0 - rate_x - rate_y - rate_z
    forward_x = ux > 0
    half = LOCAL // 2
    shift_z = jnp.where(((v >> 2) & 1) == 1, PZ - 1, 1)

    def advect(layer, c, store):
        base_block = c * BLOCKS

        def cells(at, j):
            return turned[at, :, pl.ds((j % PY) * PZ, PZ)].astype(F32)

        centre = [cells(layer + 1, base_block + j) for j in range(-1, BLOCKS + 1)]
        for j in range(BLOCKS):
            block = centre[j + 1]
            along_x = jnp.where(forward_x, cells(layer + 2, base_block + j), cells(layer, base_block + j))
            along_y = jnp.concatenate([centre[j][:half], centre[j + 2][half:]], axis=0)
            along_z = pltpu.roll(block, shift_z, 1)
            value = rest * block + rate_x * along_x + rate_y * along_y + rate_z * along_z
            store(pl.ds((base_block + j) * PZ, PZ), value.astype(BF16))

    def each(send):
        def both(codes):
            for dc in (0, 1):
                for code in codes:
                    da, db = code & 3, code >> 2
                    dx, dy = jnp.where(core == 0, da, db), jnp.where(core == 0, db, da)
                    send(device(dx, dy, dc))

        def pair(i, _):
            both([(word >> (4 * i)) & 15 for word in PACKED])
            return 0

        both([FARTHEST])
        lax.fori_loop(0, len(PAIRS), pair, 0)
        send(v ^ 1)

    own_rows = pl.ds(pl.multiple_of(v * LOCAL, LOCAL), LOCAL)

    def advect_and_send(layer, c):
        cols = chunk(c)

        def store(at, value):
            staged[layer, :, at] = value

        advect(layer, c, store)
        pltpu.make_async_remote_copy(
            src_ref=staged.at[layer, :, cols], dst_ref=mu.at[own_rows, cols], send_sem=send_sem, recv_sem=recv_sem.at[c],
            device_id={"vel": layer}, device_id_type=MESH,
        ).start()

    for c in range(CHUNKS):

        def send(layer):
            if c == 0:

                @pl.when((layer > 0) & (layer < XB - 1))
                def _():
                    advect_and_send(layer, c)
            else:
                advect_and_send(layer, c)

        each(send)
        if c == 0:

            @pl.when(g > 0)
            def _():
                to_upper().wait_recv()

            @pl.when(g < GRP - 1)
            def _():
                to_lower().wait_recv()

            for layer in (0, XB - 1):

                @pl.when(v != layer)
                def _():
                    advect_and_send(layer, 0)

    def store_own(at, value):
        mu[own_rows, at] = value

    for c in range(CHUNKS):
        advect(v, c, store_own)

    def columns(i, whole):
        at = pl.ds(pl.multiple_of(i * 128, 128), 128)
        ux, uy, uz = velocities(i * 128 + lax.broadcasted_iota(jnp.int32, (64, 128), 1))
        j = lax.broadcasted_iota(jnp.int32, (64, 128), 0)
        speed = ux * ux + uy * uy + uz * uz
        weight = jnp.exp(-speed)
        entry = poly(j & 15, ux, uy, uz) * jnp.where((j & 16) == 0, weight, weight * (speed / 3.0))
        high = entry.astype(BF16).astype(F32)
        etab[:, at] = jnp.where(j < 32, high, entry - high).astype(BF16)
        return whole + jnp.sum(weight[0:8], axis=1, keepdims=True)[0:1]

    total_weight = lax.fori_loop(0, Q // 128, columns, jnp.zeros((1, 1), F32))

    def fill(r, _):
        rows = pl.ds(pl.multiple_of(r * TABLE, TABLE), TABLE)
        ux, uy, uz = velocities(r * TABLE + lax.broadcasted_iota(jnp.int32, (TABLE, 128), 0))
        j = lax.broadcasted_iota(jnp.int32, (TABLE, 128), 1)
        absorb_tab[rows, :] = (ux * ux + uy * uy + uz * uz) / 3.0
        entry = poly(j & 15, ux, uy, uz)
        high = entry.astype(BF16).astype(F32)
        btab[rows, :] = jnp.where((j & 16) == 0, high, entry - high).astype(BF16)
        return 0

    lax.fori_loop(0, Q // TABLE, fill, 0)

    for copy in smalls:
        copy.wait()

    total[...] = jnp.zeros((VEL, 128), F32)
    def collide(c, _):
        cols = chunk(c)
        arrived = mu.at[pl.ds(0, (VEL - 1) * LOCAL), cols]
        pltpu.make_async_copy(arrived, arrived, recv_sem.at[c]).wait()
        product = jnp.dot(etab[...], mu[:, cols], preferred_element_type=F32)
        first = product[0:16] + product[32:48]
        second = product[16:32] + product[48:64]
        kind_c = kind[:, cols]
        wall = jnp.where(kind_c == 2, react[:, cols], 0.0)
        fluid = jnp.where(kind_c != 0, 1.0, 0.0)
        relax_c = relax[:, cols]

        acc = base[0, :, cols] * second[0:1]
        for k in range(1, MOMENTS):
            acc = acc + base[k, :, cols] * second[k : k + 1]
        sens = -wall * acc / total_weight
        patch_c = patch[:, cols]
        owner = lax.broadcasted_iota(jnp.int32, (VEL, WIDTH), 0) == (patch_c >> 7)
        spread = jnp.where(owner, sens, 0.0)
        piece0 = spread.astype(BF16)
        left = spread - piece0.astype(F32)
        piece1 = left.astype(BF16)
        piece2 = (left - piece1.astype(F32)).astype(BF16)
        slot = lax.broadcasted_iota(jnp.int32, (128, WIDTH), 0) == (patch_c & 15)
        sums = lax.dot_general(
            jnp.concatenate([piece0, piece1, piece2], axis=0),
            jnp.where(slot, 1.0, 0.0).astype(BF16),
            (((1,), (1,)), ((), ())),
            preferred_element_type=F32,
        )
        total[...] += sums[0:VEL] + sums[VEL : 2 * VEL] + sums[2 * VEL :]
        @pl.when(c == CHUNKS - 1)
        def _():
            for i in range(VEL):
                part[i] = total[i : i + 1]

            def give(owner):
                pltpu.make_async_remote_copy(
                    src_ref=part.at[owner], dst_ref=part_in.at[v], send_sem=psend_sem, recv_sem=precv_sem,
                    device_id={"vel": owner}, device_id_type=MESH,
                ).start()

            each(give)

        moments = (fluid * relax_c) * ((first - wall * second) / total_weight)
        high, low = split(moments)
        stacked = jnp.concatenate([high, high, low, low], axis=0)
        keep = fluid * (1.0 - relax_c)
        keep_wall = keep * wall
        def rows_of(r, _):
            rows = pl.ds(pl.multiple_of(r * ROWS, ROWS), ROWS)
            collided = jnp.dot(btab[rows, 0:64], stacked, preferred_element_type=F32)
            for j in range(WIDTH // 128):
                sub = slice(j * 128, (j + 1) * 128)
                at = pl.ds(pl.multiple_of(c * WIDTH + j * 128, 128), 128)
                factor = keep[:, sub] - keep_wall[:, sub] * absorb_tab[rows, :]
                value = factor * mu[rows, at].astype(F32) + collided[:, sub]
                result[rows, at] = value.astype(BF16)
            return 0

        lax.fori_loop(0, Q // ROWS, rows_of, 0)
        return 0

    lax.fori_loop(0, CHUNKS, collide, 0)

    part_in[pl.ds(v, 1)] = part[pl.ds(v, 1)]
    sent = part.at[pl.ds(0, VEL - 1)]
    pltpu.make_async_copy(sent, sent, precv_sem).wait()
    grad = part_in[0]
    for i in range(1, VEL):
        grad = grad + part_in[i]
    grad_out[...] = grad

    pltpu.make_async_copy(sent, sent, psend_sem).wait()
    staged_out = staged.at[pl.ds(0, VEL - 1)]
    pltpu.make_async_copy(staged_out, staged_out, send_sem).wait()

    @pl.when(g > 0)
    def _():
        to_lower().wait_send()

    @pl.when(g < GRP - 1)
    def _():
        to_upper().wait_send()


def store_kernel(result, grad, out_hbm, grad_hbm, small, out_sem, grad_sem):
    copies = []
    for c in range(STORES):
        rows = pl.ds(c * (Q // STORES), Q // STORES)
        copies.append(pltpu.make_async_copy(result.at[rows], out_hbm.at[rows], out_sem.at[c]))
    for copy in copies:
        copy.start()
    small[...] = grad[:, 0:PATCH_DEV]
    last = pltpu.make_async_copy(small, grad_hbm, grad_sem)
    last.start()
    for copy in copies:
        copy.wait()
    last.wait()


def in_hbm(x):
    return pltpu.with_memory_space_constraint(x, pltpu.HBM)


def in_vmem(x):
    return pltpu.with_memory_space_constraint(x, pltpu.VMEM)


def body(adjoint, relaxation, reaction, base_moments, cell_kind, patch_id):
    dma = pltpu.SemaphoreType.DMA
    hbm = pl.BlockSpec(memory_space=pltpu.HBM)
    vmem = pl.BlockSpec(memory_space=pltpu.VMEM)
    result, grad = pl.pallas_call(
        kernel,
        out_shape=(pltpu.VMEM((Q, CELLS), BF16), pltpu.VMEM((1, 128), F32)),
        in_specs=[hbm] * 6,
        out_specs=(vmem, vmem),
        scratch_shapes=[
            pltpu.VMEM((LOCAL, XB, CELLS), BF16),
            pltpu.VMEM((XB + 2, LOCAL, CELLS), BF16),
            pltpu.VMEM((XB, LOCAL, CELLS), BF16),
            pltpu.VMEM((Q, CELLS), BF16),
            pltpu.VMEM((1, CELLS), F32),
            pltpu.VMEM((1, CELLS), F32),
            pltpu.VMEM((MOMENTS, 1, CELLS), F32),
            pltpu.VMEM((1, CELLS), jnp.int32),
            pltpu.VMEM((1, CELLS), jnp.int32),
            pltpu.VMEM((Q, 128), F32),
            pltpu.VMEM((64, Q), BF16),
            pltpu.VMEM((Q, 128), BF16),
            pltpu.VMEM((VEL, 1, 128), F32),
            pltpu.VMEM((VEL, 1, 128), F32),
            pltpu.VMEM((VEL, 128), F32),
            dma((CHUNKS,)),
            dma((5,)),
            dma((2,)),
            dma((2,)),
            dma,
            dma((CHUNKS,)),
            dma,
            dma,
        ],
        compiler_params=pltpu.CompilerParams(
            collective_id=0, has_side_effects=True, vmem_limit_bytes=40 * 1024 * 1024
        ),
        name="adjoint_step",
    )(*[in_hbm(x) for x in (adjoint, relaxation, reaction, base_moments, cell_kind, patch_id)])
    out, grad = pl.pallas_call(
        store_kernel,
        out_shape=(jax.ShapeDtypeStruct((Q, CELLS), BF16), jax.ShapeDtypeStruct((1, PATCH_DEV), F32)),
        in_specs=[vmem] * 2,
        out_specs=(hbm, hbm),
        scratch_shapes=[pltpu.VMEM((1, PATCH_DEV), F32), dma((STORES,)), dma],
        compiler_params=pltpu.CompilerParams(vmem_limit_bytes=8 * 1024 * 1024),
        name="store_step",
    )(in_vmem(result), in_vmem(grad))
    return out.reshape(Q, 1, 1, CELLS), grad.reshape(PATCH_DEV)


def solution(mesh):
    placed = (
        P("vel", "grp", None, None),
        P("grp", "vel", None),
        P("grp", "vel", None),
        P(None, "grp", "vel", None),
        P("grp", "vel", None),
        P("grp", "vel", None),
    )
    return jax.shard_map(
        body,
        mesh=mesh,
        in_specs=placed,
        out_specs=(P(None, "grp", "vel", None), P(("vel", "grp"))),
        check_vma=False,
    )
```

```python
import jax
import jax.numpy as jnp
from jax import lax
from jax.experimental import pallas as pl
from jax.experimental.pallas import tpu as pltpu
from jax.sharding import PartitionSpec as P

NV = 8
MOMENTS = 10
PY = 16
PZ = 128
PATCH_DEV = 16
Q = 512
XB = 32
CELLS = PY * PZ
COURANT = 0.3

VEL = 32
GRP = 8
LOCAL = Q // VEL
CHUNKS = 4
WIDTH = CELLS // CHUNKS
STARTS = (0, 512, 1024, 1536, 1664)
SIZES = (512, 512, 512, 128, 384)
LAST = len(SIZES) - 1
GROUPS = SIZES[LAST] // PZ
SUMS = 5
PAIRS = ((6, 14), (9, 11), (5, 15), (13, 7), (2, 8), (1, 3), (4, 12))
FARTHEST = 10
NEAR = 2
PACKED = tuple(sum(pair[member] << (4 * i) for i, pair in enumerate(PAIRS)) for member in (0, 1))
ROWS = 128
TABLE = 32
STORES = 4

MESH = pl.DeviceIdType.MESH
F32 = jnp.float32
BF16 = jnp.bfloat16


def component(digit):
    sign = jnp.where((digit & 1) == 0, -1.0, 1.0).astype(F32)
    return sign * ((digit >> 1).astype(F32) + 0.5) / (NV / 2.0 - 0.5)


def velocities(vel_index):
    return (
        component(vel_index & (NV - 1)),
        component((vel_index >> 3) & (NV - 1)),
        component(vel_index >> 6),
    )


def poly(k, ux, uy, uz):
    third = 1.0 / 3.0
    terms = (
        jnp.ones_like(ux),
        ux,
        uy,
        uz,
        ux * ux - third,
        uy * uy - third,
        uz * uz - third,
        ux * uy,
        ux * uz,
        uy * uz,
    )
    value = jnp.zeros_like(ux)
    for i, term in enumerate(terms):
        value = jnp.where(k == i, term, value)
    return value


def split(value):
    high = value.astype(BF16)
    return high, (value - high.astype(F32)).astype(BF16)


def kernel(
    adj_hbm, relax_hbm, react_hbm, base_hbm, kind_hbm, patch_hbm,
    result, grad_out,
    xin, turned, staged, mu, relax, react, base, kind, patch,
    absorb_tab, etab, btab, part, part_in, total, sums_out, sums_in, back,
    round_sem, sums_sem, load_sem, small_sem, halo_send, halo_recv, send_sem, recv_sem, psend_sem, precv_sem,
):
    v = lax.axis_index("vel")
    g = lax.axis_index("grp")
    core = v & 1

    def chunk(c):
        return pl.ds(c * WIDTH, WIDTH) if isinstance(c, int) else pl.ds(pl.multiple_of(c * WIDTH, WIDTH), WIDTH)

    def part_of(c):
        return pl.ds(STARTS[c], SIZES[c])

    def load(i):
        return pltpu.make_async_copy(adj_hbm.at[:, 0, :, chunk(i)], xin.at[:, :, chunk(i)], load_sem.at[i])

    for i in range(CHUNKS):
        load(i).start()
    smalls = [
        pltpu.make_async_copy(relax_hbm.at[0], relax, small_sem.at[0]),
        pltpu.make_async_copy(react_hbm.at[0], react, small_sem.at[1]),
        pltpu.make_async_copy(kind_hbm.at[0], kind, small_sem.at[2]),
        pltpu.make_async_copy(patch_hbm.at[0], patch, small_sem.at[3]),
        pltpu.make_async_copy(base_hbm.at[:, 0], base, small_sem.at[4]),
    ]
    for copy in smalls:
        copy.start()

    def device(dx, dy, dc):
        y, x = v >> 3, (v >> 1) & 3
        return (((y + dy) & 3) << 3) + (((x + dx) & 3) << 1) + ((core + dc) & 1)

    barrier = pltpu.get_barrier_semaphore()
    pl.semaphore_signal(barrier, inc=1, device_id={"vel": v ^ 1}, device_id_type=MESH)
    for code in sum(PAIRS[NEAR:], ()):
        for dc in (0, 1):
            near = device(code & 3, code >> 2, dc)
            pl.semaphore_signal(barrier, inc=1, device_id={"vel": near}, device_id_type=MESH)

    @pl.when(g > 0)
    def _():
        pl.semaphore_signal(barrier, inc=1, device_id={"grp": g - 1}, device_id_type=MESH)

    @pl.when(g < GRP - 1)
    def _():
        pl.semaphore_signal(barrier, inc=1, device_id={"grp": g + 1}, device_id_type=MESH)

    for i in range(CHUNKS):
        load(i).wait()
        for t in range(XB // 16):
            block = xin[:, pl.ds(16 * t, 16), chunk(i)]
            turned[pl.ds(1 + 16 * t, 16), :, chunk(i)] = jnp.swapaxes(block, 0, 1)

    neighbours = jnp.where(g > 0, 1, 0) + jnp.where(g < GRP - 1, 1, 0)
    pl.semaphore_wait(barrier, 1 + 4 * (len(PAIRS) - NEAR) + neighbours)
    for dx, dy in ((2, 0), (0, 2)):
        pl.semaphore_signal(round_sem, inc=1, device_id={"vel": device(dx, dy, 0)}, device_id_type=MESH)

    def to_lower():
        return pltpu.make_async_remote_copy(
            src_ref=turned.at[1], dst_ref=turned.at[XB + 1], send_sem=halo_send.at[0], recv_sem=halo_recv.at[0],
            device_id={"grp": g - 1}, device_id_type=MESH,
        )

    def to_upper():
        return pltpu.make_async_remote_copy(
            src_ref=turned.at[XB], dst_ref=turned.at[0], send_sem=halo_send.at[1], recv_sem=halo_recv.at[1],
            device_id={"grp": g + 1}, device_id_type=MESH,
        )

    @pl.when(g > 0)
    def _():
        to_lower().start()

    @pl.when(g < GRP - 1)
    def _():
        to_upper().start()

    @pl.when(g == 0)
    def _():
        turned[0] = jnp.zeros((LOCAL, CELLS), BF16)

    @pl.when(g == GRP - 1)
    def _():
        turned[XB + 1] = jnp.zeros((LOCAL, CELLS), BF16)

    own = v * LOCAL + lax.broadcasted_iota(jnp.int32, (LOCAL, PZ), 0)
    ux, uy, uz = velocities(own)
    rate_x, rate_y, rate_z = COURANT * jnp.abs(ux), COURANT * jnp.abs(uy), COURANT * jnp.abs(uz)
    rest = 1.0 - rate_x - rate_y - rate_z
    forward_x = ux > 0
    half = LOCAL // 2
    shift_z = jnp.where(((v >> 2) & 1) == 1, PZ - 1, 1)

    def advect(layer, c, store):
        base_block, count = STARTS[c] // PZ, SIZES[c] // PZ

        def cells(at, j):
            return turned[at, :, pl.ds((j % PY) * PZ, PZ)].astype(F32)

        centre = [cells(layer + 1, base_block + j) for j in range(-1, count + 1)]
        for j in range(count):
            block = centre[j + 1]
            along_x = jnp.where(forward_x, cells(layer + 2, base_block + j), cells(layer, base_block + j))
            along_y = jnp.concatenate([centre[j][:half], centre[j + 2][half:]], axis=0)
            along_z = pltpu.roll(block, shift_z, 1)
            value = rest * block + rate_x * along_x + rate_y * along_y + rate_z * along_z
            store(pl.ds((base_block + j) * PZ, PZ), value.astype(BF16))

    def both(codes, send):
        for dc in (0, 1):
            for code in codes:
                da, db = code & 3, code >> 2
                dx, dy = jnp.where(core == 0, da, db), jnp.where(core == 0, db, da)
                send(device(dx, dy, dc))

    def pairs(first, last, send):
        def pair(i, _):
            both([(word >> (4 * i)) & 15 for word in PACKED], send)
            return 0

        lax.fori_loop(first, last, pair, 0)

    def far(send):
        both([FARTHEST], send)
        pairs(0, NEAR, send)

    def each(send):
        both([FARTHEST], send)
        pairs(0, len(PAIRS), send)
        send(v ^ 1)

    own_rows = pl.ds(pl.multiple_of(v * LOCAL, LOCAL), LOCAL)

    def advect_here(layer, c):
        def store(at, value):
            staged[layer, :, at] = value

        advect(layer, c, store)

    def send_part(layer, c):
        pltpu.make_async_remote_copy(
            src_ref=staged.at[layer, :, part_of(c)], dst_ref=mu.at[own_rows, part_of(c)],
            send_sem=send_sem, recv_sem=recv_sem.at[c], device_id={"vel": layer}, device_id_type=MESH,
        ).start()

    def advect_and_send(layer, c):
        advect_here(layer, c)
        send_part(layer, c)

    def inner(layer):
        @pl.when((layer > 0) & (layer < XB - 1))
        def _():
            advect_and_send(layer, 0)

    pairs(NEAR, len(PAIRS), inner)
    inner(v ^ 1)
    pl.semaphore_wait(round_sem, 2)
    far(inner)

    @pl.when(g > 0)
    def _():
        to_upper().wait_recv()

    @pl.when(g < GRP - 1)
    def _():
        to_lower().wait_recv()

    for layer in (0, XB - 1):

        @pl.when(v != layer)
        def _():
            advect_and_send(layer, 0)

    for c in range(1, LAST):
        each(lambda layer: advect_and_send(layer, c))

    lax.fori_loop(0, XB, lambda layer, _: (advect_here(layer, LAST), 0)[1], 0)
    r_at = lax.broadcasted_iota(jnp.int32, (LOCAL, 256), 0)
    q_at = lax.broadcasted_iota(jnp.int32, (LOCAL, 256), 1)
    ux, uy, uz = velocities(v * LOCAL + (q_at & 15))
    speed = ux * ux + uy * uy + uz * uz
    weight = jnp.exp(-speed) * (speed / 3.0)
    signed = jnp.where(uy > 0, weight, -weight)
    factors = (weight, weight * ux, weight * ux * ux, signed, signed * ux)
    same = (lax.broadcasted_iota(jnp.int32, (256, 256), 0) >> 4) == (lax.broadcasted_iota(jnp.int32, (256, 256), 1) >> 4)
    tables = []
    for j in range(GROUPS):
        entry = jnp.zeros((LOCAL, 256), F32)
        for i, factor in enumerate(factors):
            entry = jnp.where(r_at == SUMS * j + i, factor, entry)
        for piece in split(entry):
            whole = jnp.concatenate([piece.astype(F32)] * 16, axis=0)
            tables.append((j, jnp.where(same, whole, 0.0).astype(BF16)))
    for t in range(XB // 16):
        acc = jnp.zeros((256, PZ), F32)
        for j, table in tables:
            block = staged[pl.ds(16 * t, 16), :, pl.ds(STARTS[LAST] + j * PZ, PZ)].reshape(256, PZ)
            acc = acc + jnp.dot(table, block, preferred_element_type=F32)
        sums_out[pl.ds(256 * t, 256), :] = acc.astype(BF16)

    def send_sums(layer):
        pltpu.make_async_remote_copy(
            src_ref=sums_out.at[pl.ds(pl.multiple_of(layer * LOCAL, LOCAL), LOCAL)], dst_ref=sums_in.at[own_rows],
            send_sem=sums_sem.at[0], recv_sem=sums_sem.at[1], device_id={"vel": layer}, device_id_type=MESH,
        ).start()

    each(send_sums)
    sums_in[own_rows, :] = sums_out[own_rows, :]
    each(lambda layer: send_part(layer, LAST))

    def store_own(at, value):
        mu[own_rows, at] = value

    for c in range(len(SIZES)):
        advect(v, c, store_own)

    def columns(i, whole):
        at = pl.ds(pl.multiple_of(i * 128, 128), 128)
        ux, uy, uz = velocities(i * 128 + lax.broadcasted_iota(jnp.int32, (64, 128), 1))
        j = lax.broadcasted_iota(jnp.int32, (64, 128), 0)
        speed = ux * ux + uy * uy + uz * uz
        weight = jnp.exp(-speed)
        entry = poly(j & 15, ux, uy, uz) * jnp.where((j & 16) == 0, weight, weight * (speed / 3.0))
        high = entry.astype(BF16).astype(F32)
        etab[:, at] = jnp.where(j < 32, high, entry - high).astype(BF16)
        return whole + jnp.sum(weight[0:8], axis=1, keepdims=True)[0:1]

    total_weight = lax.fori_loop(0, Q // 128, columns, jnp.zeros((1, 1), F32))

    def fill(r, _):
        rows = pl.ds(pl.multiple_of(r * TABLE, TABLE), TABLE)
        ux, uy, uz = velocities(r * TABLE + lax.broadcasted_iota(jnp.int32, (TABLE, 128), 0))
        j = lax.broadcasted_iota(jnp.int32, (TABLE, 128), 1)
        absorb_tab[rows, :] = (ux * ux + uy * uy + uz * uz) / 3.0
        entry = poly(j & 15, ux, uy, uz)
        high = entry.astype(BF16).astype(F32)
        btab[rows, :] = jnp.where((j & 16) == 0, high, entry - high).astype(BF16)
        return 0

    lax.fori_loop(0, Q // TABLE, fill, 0)

    r_at = lax.broadcasted_iota(jnp.int32, (GROUPS * 16, Q), 0)
    q_at = lax.broadcasted_iota(jnp.int32, (GROUPS * 16, Q), 1)
    k_at, i_at = r_at & 15, (q_at & 15) - SUMS * (r_at >> 4)
    third = 1.0 / 3.0
    side = jnp.abs(component(((q_at >> 4) & 3) * 2))
    uz = component(q_at >> 6)
    entry = jnp.zeros((GROUPS * 16, Q), F32)
    for k, i, value in (
        (0, 0, 1.0), (1, 1, 1.0), (2, 3, side), (3, 0, uz), (4, 2, 1.0), (4, 0, -third), (5, 0, side * side - third),
        (6, 0, uz * uz - third), (7, 4, side), (8, 1, uz), (9, 3, uz * side),
    ):
        entry = jnp.where((k_at == k) & (i_at == i), value, entry)
    high, low = split(entry)
    back[...] = jnp.concatenate([high, low], axis=0)

    for copy in smalls:
        copy.wait()

    total[...] = jnp.zeros((VEL, 128), F32)

    def arrive(c, cols):
        arrived = mu.at[pl.ds(0, (VEL - 1) * LOCAL), cols]
        pltpu.make_async_copy(arrived, arrived, recv_sem.at[c]).wait()

    def project(cols):
        product = jnp.dot(etab[...], mu[:, cols], preferred_element_type=F32)
        return product[0:16] + product[32:48], product[16:32] + product[48:64]

    def wall_of(cols):
        return jnp.where(kind[:, cols] == 2, react[:, cols], 0.0)

    def add_patches(cols, second):
        acc = base[0, :, cols] * second[0:1]
        for k in range(1, MOMENTS):
            acc = acc + base[k, :, cols] * second[k : k + 1]
        sens = -wall_of(cols) * acc / total_weight
        patch_c = patch[:, cols]
        owner = lax.broadcasted_iota(jnp.int32, (VEL, WIDTH), 0) == (patch_c >> 7)
        spread = jnp.where(owner, sens, 0.0)
        piece0 = spread.astype(BF16)
        left = spread - piece0.astype(F32)
        piece1 = left.astype(BF16)
        piece2 = (left - piece1.astype(F32)).astype(BF16)
        slot = lax.broadcasted_iota(jnp.int32, (128, WIDTH), 0) == (patch_c & 15)
        sums = lax.dot_general(
            jnp.concatenate([piece0, piece1, piece2], axis=0),
            jnp.where(slot, 1.0, 0.0).astype(BF16),
            (((1,), (1,)), ((), ())),
            preferred_element_type=F32,
        )
        total[...] += sums[0:VEL] + sums[VEL : 2 * VEL] + sums[2 * VEL :]

    def relax_cells(c, first, second):
        cols = chunk(c)
        wall = wall_of(cols)
        fluid = jnp.where(kind[:, cols] != 0, 1.0, 0.0)
        relax_c = relax[:, cols]
        moments = (fluid * relax_c) * ((first - wall * second) / total_weight)
        high, low = split(moments)
        stacked = jnp.concatenate([high, high, low, low], axis=0)
        keep = fluid * (1.0 - relax_c)
        keep_wall = keep * wall

        def rows_of(r, _):
            rows = pl.ds(pl.multiple_of(r * ROWS, ROWS), ROWS)
            collided = jnp.dot(btab[rows, 0:64], stacked, preferred_element_type=F32)
            for j in range(WIDTH // 128):
                sub = slice(j * 128, (j + 1) * 128)
                at = pl.ds(pl.multiple_of(c * WIDTH + j * 128, 128), 128)
                factor = keep[:, sub] - keep_wall[:, sub] * absorb_tab[rows, :]
                value = factor * mu[rows, at].astype(F32) + collided[:, sub]
                result[rows, at] = value.astype(BF16)
            return 0

        lax.fori_loop(0, Q // ROWS, rows_of, 0)

    def step(c, _):
        cols = chunk(c)

        @pl.when(c < CHUNKS - 1)
        def _():
            arrive(c, cols)
            first, second = project(cols)
            add_patches(cols, second)
            relax_cells(c, first, second)

        @pl.when(c == CHUNKS - 1)
        def _():
            arrive(LAST - 1, part_of(LAST - 1))
            _, second = project(part_of(LAST - 1))
            came = sums_in.at[pl.ds(0, (VEL - 1) * LOCAL)]
            pltpu.make_async_copy(came, came, sums_sem.at[1]).wait()
            product = jnp.dot(back[...], sums_in[...], preferred_element_type=F32)
            later = [
                product[16 * j : 16 * (j + 1)] + product[16 * (GROUPS + j) : 16 * (GROUPS + j + 1)]
                for j in range(GROUPS)
            ]
            add_patches(cols, jnp.concatenate([second] + later, axis=1))
            for i in range(VEL):
                part[i] = total[i : i + 1]

            def give(owner):
                pltpu.make_async_remote_copy(
                    src_ref=part.at[owner], dst_ref=part_in.at[v], send_sem=psend_sem, recv_sem=precv_sem,
                    device_id={"vel": owner}, device_id_type=MESH,
                ).start()

            each(give)
            arrive(LAST, part_of(LAST))
            first, second = project(cols)
            relax_cells(c, first, second)

        return 0

    lax.fori_loop(0, CHUNKS, step, 0)

    part_in[pl.ds(v, 1)] = part[pl.ds(v, 1)]
    sent = part.at[pl.ds(0, VEL - 1)]
    pltpu.make_async_copy(sent, sent, precv_sem).wait()
    grad = part_in[0]
    for i in range(1, VEL):
        grad = grad + part_in[i]
    grad_out[...] = grad

    pltpu.make_async_copy(sent, sent, psend_sem).wait()
    gone = sums_out.at[pl.ds(0, (VEL - 1) * LOCAL)]
    pltpu.make_async_copy(gone, gone, sums_sem.at[0]).wait()
    staged_out = staged.at[pl.ds(0, VEL - 1)]
    pltpu.make_async_copy(staged_out, staged_out, send_sem).wait()

    @pl.when(g > 0)
    def _():
        to_lower().wait_send()

    @pl.when(g < GRP - 1)
    def _():
        to_upper().wait_send()


def store_kernel(result, grad, out_hbm, grad_hbm, small, out_sem, grad_sem):
    copies = []
    for c in range(STORES):
        rows = pl.ds(c * (Q // STORES), Q // STORES)
        copies.append(pltpu.make_async_copy(result.at[rows], out_hbm.at[rows], out_sem.at[c]))
    for copy in copies:
        copy.start()
    small[...] = grad[:, 0:PATCH_DEV]
    last = pltpu.make_async_copy(small, grad_hbm, grad_sem)
    last.start()
    for copy in copies:
        copy.wait()
    last.wait()


def in_hbm(x):
    return pltpu.with_memory_space_constraint(x, pltpu.HBM)


def in_vmem(x):
    return pltpu.with_memory_space_constraint(x, pltpu.VMEM)


def body(adjoint, relaxation, reaction, base_moments, cell_kind, patch_id):
    dma = pltpu.SemaphoreType.DMA
    hbm = pl.BlockSpec(memory_space=pltpu.HBM)
    vmem = pl.BlockSpec(memory_space=pltpu.VMEM)
    result, grad = pl.pallas_call(
        kernel,
        out_shape=(pltpu.VMEM((Q, CELLS), BF16), pltpu.VMEM((1, 128), F32)),
        in_specs=[hbm] * 6,
        out_specs=(vmem, vmem),
        scratch_shapes=[
            pltpu.VMEM((LOCAL, XB, CELLS), BF16),
            pltpu.VMEM((XB + 2, LOCAL, CELLS), BF16),
            pltpu.VMEM((XB, LOCAL, CELLS), BF16),
            pltpu.VMEM((Q, CELLS), BF16),
            pltpu.VMEM((1, CELLS), F32),
            pltpu.VMEM((1, CELLS), F32),
            pltpu.VMEM((MOMENTS, 1, CELLS), F32),
            pltpu.VMEM((1, CELLS), jnp.int32),
            pltpu.VMEM((1, CELLS), jnp.int32),
            pltpu.VMEM((Q, 128), F32),
            pltpu.VMEM((64, Q), BF16),
            pltpu.VMEM((Q, 128), BF16),
            pltpu.VMEM((VEL, 1, 128), F32),
            pltpu.VMEM((VEL, 1, 128), F32),
            pltpu.VMEM((VEL, 128), F32),
            pltpu.VMEM((Q, PZ), BF16),
            pltpu.VMEM((Q, PZ), BF16),
            pltpu.VMEM((2 * GROUPS * 16, Q), BF16),
            pltpu.SemaphoreType.REGULAR,
            dma((2,)),
            dma((CHUNKS,)),
            dma((5,)),
            dma((2,)),
            dma((2,)),
            dma,
            dma((len(SIZES),)),
            dma,
            dma,
        ],
        compiler_params=pltpu.CompilerParams(
            collective_id=0, has_side_effects=True, vmem_limit_bytes=40 * 1024 * 1024
        ),
        name="adjoint_step",
    )(*[in_hbm(x) for x in (adjoint, relaxation, reaction, base_moments, cell_kind, patch_id)])
    out, grad = pl.pallas_call(
        store_kernel,
        out_shape=(jax.ShapeDtypeStruct((Q, CELLS), BF16), jax.ShapeDtypeStruct((1, PATCH_DEV), F32)),
        in_specs=[vmem] * 2,
        out_specs=(hbm, hbm),
        scratch_shapes=[pltpu.VMEM((1, PATCH_DEV), F32), dma((STORES,)), dma],
        compiler_params=pltpu.CompilerParams(vmem_limit_bytes=8 * 1024 * 1024),
        name="store_step",
    )(in_vmem(result), in_vmem(grad))
    return out.reshape(Q, 1, 1, CELLS), grad.reshape(PATCH_DEV)


def solution(mesh):
    placed = (
        P("vel", "grp", None, None),
        P("grp", "vel", None),
        P("grp", "vel", None),
        P(None, "grp", "vel", None),
        P("grp", "vel", None),
        P("grp", "vel", None),
    )
    return jax.shard_map(
        body,
        mesh=mesh,
        in_specs=placed,
        out_specs=(P(None, "grp", "vel", None), P(("vel", "grp"))),
        check_vma=False,
    )
```

```python
import jax
import jax.numpy as jnp
from jax import lax
from jax.experimental import pallas as pl
from jax.experimental.pallas import tpu as pltpu
from jax.sharding import PartitionSpec as P

NV = 8
MOMENTS = 10
PY = 16
PZ = 128
PATCH_DEV = 16
Q = 512
XB = 32
CELLS = PY * PZ
COURANT = 0.3

VEL = 32
GRP = 8
LOCAL = Q // VEL
CHUNKS = 4
WIDTH = CELLS // CHUNKS
BLOCKS = WIDTH // PZ
PAIRS = ((6, 14), (9, 11), (5, 15), (13, 7), (2, 8), (1, 3), (4, 12))
FARTHEST = 10
NEAR = 2
STRIDE = 13
PACKED = tuple(sum(pair[member] << (4 * i) for i, pair in enumerate(PAIRS)) for member in (0, 1))
ROWS = 128
TABLE = 32
STORES = 4

MESH = pl.DeviceIdType.MESH
F32 = jnp.float32
BF16 = jnp.bfloat16


def component(digit):
    sign = jnp.where((digit & 1) == 0, -1.0, 1.0).astype(F32)
    return sign * ((digit >> 1).astype(F32) + 0.5) / (NV / 2.0 - 0.5)


def velocities(vel_index):
    return (
        component(vel_index & (NV - 1)),
        component((vel_index >> 3) & (NV - 1)),
        component(vel_index >> 6),
    )


def poly(k, ux, uy, uz):
    third = 1.0 / 3.0
    terms = (
        jnp.ones_like(ux),
        ux,
        uy,
        uz,
        ux * ux - third,
        uy * uy - third,
        uz * uz - third,
        ux * uy,
        ux * uz,
        uy * uz,
    )
    value = jnp.zeros_like(ux)
    for i, term in enumerate(terms):
        value = jnp.where(k == i, term, value)
    return value


def split(value):
    high = value.astype(BF16)
    return high, (value - high.astype(F32)).astype(BF16)


def kernel(
    adj_hbm, relax_hbm, react_hbm, base_hbm, kind_hbm, patch_hbm,
    result, grad_out,
    xin, turned, staged, mu, relax, react, base, kind, patch,
    absorb_tab, etab, btab, part, part_in, total, coef, slots,
    round_sem, load_sem, small_sem, halo_send, halo_recv, send_sem, recv_sem, psend_sem, precv_sem,
):
    v = lax.axis_index("vel")
    g = lax.axis_index("grp")
    core = v & 1

    def chunk(c):
        return pl.ds(c * WIDTH, WIDTH) if isinstance(c, int) else pl.ds(pl.multiple_of(c * WIDTH, WIDTH), WIDTH)

    def load(i):
        return pltpu.make_async_copy(adj_hbm.at[:, 0, :, chunk(i)], xin.at[:, :, chunk(i)], load_sem.at[i])

    for i in range(CHUNKS):
        load(i).start()
    smalls = [
        pltpu.make_async_copy(relax_hbm.at[0], relax, small_sem.at[0]),
        pltpu.make_async_copy(react_hbm.at[0], react, small_sem.at[1]),
        pltpu.make_async_copy(kind_hbm.at[0], kind, small_sem.at[2]),
        pltpu.make_async_copy(patch_hbm.at[0], patch, small_sem.at[3]),
        pltpu.make_async_copy(base_hbm.at[:, 0], base, small_sem.at[4]),
    ]
    for copy in smalls:
        copy.start()

    def device(dx, dy, dc):
        y, x = v >> 3, (v >> 1) & 3
        return (((y + dy) & 3) << 3) + (((x + dx) & 3) << 1) + ((core + dc) & 1)

    barrier = pltpu.get_barrier_semaphore()
    pl.semaphore_signal(barrier, inc=1, device_id={"vel": v ^ 1}, device_id_type=MESH)
    for code in sum(PAIRS[NEAR:], ()):
        for dc in (0, 1):
            near = device(code & 3, code >> 2, dc)
            pl.semaphore_signal(barrier, inc=1, device_id={"vel": near}, device_id_type=MESH)

    @pl.when(g > 0)
    def _():
        pl.semaphore_signal(barrier, inc=1, device_id={"grp": g - 1}, device_id_type=MESH)

    @pl.when(g < GRP - 1)
    def _():
        pl.semaphore_signal(barrier, inc=1, device_id={"grp": g + 1}, device_id_type=MESH)

    for i in range(CHUNKS):
        load(i).wait()
        for t in range(XB // 16):
            block = xin[:, pl.ds(16 * t, 16), chunk(i)]
            turned[pl.ds(1 + 16 * t, 16), :, chunk(i)] = jnp.swapaxes(block, 0, 1)

    neighbours = jnp.where(g > 0, 1, 0) + jnp.where(g < GRP - 1, 1, 0)
    pl.semaphore_wait(barrier, 1 + 4 * (len(PAIRS) - NEAR) + neighbours)
    for dx, dy in ((2, 0), (0, 2)):
        pl.semaphore_signal(round_sem, inc=1, device_id={"vel": device(dx, dy, 0)}, device_id_type=MESH)

    def to_lower():
        return pltpu.make_async_remote_copy(
            src_ref=turned.at[1], dst_ref=turned.at[XB + 1], send_sem=halo_send.at[0], recv_sem=halo_recv.at[0],
            device_id={"grp": g - 1}, device_id_type=MESH,
        )

    def to_upper():
        return pltpu.make_async_remote_copy(
            src_ref=turned.at[XB], dst_ref=turned.at[0], send_sem=halo_send.at[1], recv_sem=halo_recv.at[1],
            device_id={"grp": g + 1}, device_id_type=MESH,
        )

    @pl.when(g > 0)
    def _():
        to_lower().start()

    @pl.when(g < GRP - 1)
    def _():
        to_upper().start()

    @pl.when(g == 0)
    def _():
        turned[0] = jnp.zeros((LOCAL, CELLS), BF16)

    @pl.when(g == GRP - 1)
    def _():
        turned[XB + 1] = jnp.zeros((LOCAL, CELLS), BF16)

    own = v * LOCAL + lax.broadcasted_iota(jnp.int32, (LOCAL, PZ), 0)
    ux, uy, uz = velocities(own)
    rate_x, rate_y, rate_z = COURANT * jnp.abs(ux), COURANT * jnp.abs(uy), COURANT * jnp.abs(uz)
    rest = 1.0 - rate_x - rate_y - rate_z
    forward_x = ux > 0
    half = LOCAL // 2
    shift_z = jnp.where(((v >> 2) & 1) == 1, PZ - 1, 1)

    def advect(layer, c, store):
        base_block = c * BLOCKS

        def cells(at, j):
            return turned[at, :, pl.ds((j % PY) * PZ, PZ)].astype(F32)

        centre = [cells(layer + 1, base_block + j) for j in range(-1, BLOCKS + 1)]
        for j in range(BLOCKS):
            block = centre[j + 1]
            along_x = jnp.where(forward_x, cells(layer + 2, base_block + j), cells(layer, base_block + j))
            along_y = jnp.concatenate([centre[j][:half], centre[j + 2][half:]], axis=0)
            along_z = pltpu.roll(block, shift_z, 1)
            value = rest * block + rate_x * along_x + rate_y * along_y + rate_z * along_z
            store(pl.ds((base_block + j) * PZ, PZ), value.astype(BF16))

    def both(codes, send):
        for dc in (0, 1):
            for code in codes:
                da, db = code & 3, code >> 2
                dx, dy = jnp.where(core == 0, da, db), jnp.where(core == 0, db, da)
                send(device(dx, dy, dc))

    def pairs(first, last, send):
        def pair(i, _):
            both([(word >> (4 * i)) & 15 for word in PACKED], send)
            return 0

        lax.fori_loop(first, last, pair, 0)

    def far(send):
        both([FARTHEST], send)
        pairs(0, NEAR, send)

    def each(send):
        both([FARTHEST], send)
        pairs(0, len(PAIRS), send)
        send(v ^ 1)

    own_rows = pl.ds(pl.multiple_of(v * LOCAL, LOCAL), LOCAL)

    def advect_and_send(layer, c):
        cols = chunk(c)

        def store(at, value):
            staged[layer, :, at] = value

        advect(layer, c, store)
        pltpu.make_async_remote_copy(
            src_ref=staged.at[layer, :, cols], dst_ref=mu.at[own_rows, cols], send_sem=send_sem, recv_sem=recv_sem.at[c],
            device_id={"vel": layer}, device_id_type=MESH,
        ).start()

    def inner(layer):
        @pl.when((layer > 0) & (layer < XB - 1))
        def _():
            advect_and_send(layer, 0)

    pairs(NEAR, len(PAIRS), inner)
    inner(v ^ 1)
    pl.semaphore_wait(round_sem, 2)
    far(inner)

    @pl.when(g > 0)
    def _():
        to_upper().wait_recv()

    @pl.when(g < GRP - 1)
    def _():
        to_lower().wait_recv()

    for layer in (0, XB - 1):

        @pl.when(v != layer)
        def _():
            advect_and_send(layer, 0)

    for c in range(1, CHUNKS):
        each(lambda layer: advect_and_send(layer, c))

    def store_own(at, value):
        mu[own_rows, at] = value

    for c in range(CHUNKS):
        advect(v, c, store_own)

    def columns(i, whole):
        at = pl.ds(pl.multiple_of(i * 128, 128), 128)
        ux, uy, uz = velocities(i * 128 + lax.broadcasted_iota(jnp.int32, (64, 128), 1))
        j = lax.broadcasted_iota(jnp.int32, (64, 128), 0)
        speed = ux * ux + uy * uy + uz * uz
        weight = jnp.exp(-speed)
        entry = poly(j & 15, ux, uy, uz) * jnp.where((j & 16) == 0, weight, weight * (speed / 3.0))
        high = entry.astype(BF16).astype(F32)
        etab[:, at] = jnp.where(j < 32, high, entry - high).astype(BF16)
        return whole + jnp.sum(weight[0:8], axis=1, keepdims=True)[0:1]

    total_weight = lax.fori_loop(0, Q // 128, columns, jnp.zeros((1, 1), F32))

    def fill(r, _):
        rows = pl.ds(pl.multiple_of(r * TABLE, TABLE), TABLE)
        ux, uy, uz = velocities(r * TABLE + lax.broadcasted_iota(jnp.int32, (TABLE, 128), 0))
        j = lax.broadcasted_iota(jnp.int32, (TABLE, 128), 1)
        absorb_tab[rows, :] = (ux * ux + uy * uy + uz * uz) / 3.0
        entry = poly(j & 15, ux, uy, uz)
        high = entry.astype(BF16).astype(F32)
        btab[rows, :] = jnp.where((j & 16) == 0, high, entry - high).astype(BF16)
        return 0

    lax.fori_loop(0, Q // TABLE, fill, 0)

    for copy in smalls:
        copy.wait()

    coef[...] = jnp.zeros((16, CELLS), F32)
    scale = -jnp.where(kind[...] == 2, react[...], 0.0) / total_weight
    for k in range(MOMENTS):
        coef[k : k + 1, :] = scale * base[k]
    for c in range(CHUNKS):
        slot = lax.broadcasted_iota(jnp.int32, (128, WIDTH), 0) == (patch[:, chunk(c)] & 15)
        slots[:, chunk(c)] = jnp.where(slot, 1.0, 0.0).astype(BF16)

    total[...] = jnp.zeros((VEL, 128), F32)

    def collide(c, _):
        cols = chunk(c)
        arrived = mu.at[pl.ds(0, (VEL - 1) * LOCAL), cols]
        pltpu.make_async_copy(arrived, arrived, recv_sem.at[c]).wait()
        product = jnp.dot(etab[...], mu[:, cols], preferred_element_type=F32)
        first = product[0:16] + product[32:48]
        second = product[16:32] + product[48:64]
        kind_c = kind[:, cols]
        wall = jnp.where(kind_c == 2, react[:, cols], 0.0)
        fluid = jnp.where(kind_c != 0, 1.0, 0.0)
        relax_c = relax[:, cols]

        sens = jnp.sum(coef[:, cols] * second, axis=0, keepdims=True)
        patch_c = patch[:, cols]
        owner = lax.broadcasted_iota(jnp.int32, (VEL, WIDTH), 0) == (patch_c >> 7)
        spread = jnp.where(owner, sens, 0.0)
        piece0 = spread.astype(BF16)
        left = spread - piece0.astype(F32)
        piece1 = left.astype(BF16)
        piece2 = (left - piece1.astype(F32)).astype(BF16)
        sums = lax.dot_general(
            jnp.concatenate([piece0, piece1, piece2], axis=0),
            slots[:, cols],
            (((1,), (1,)), ((), ())),
            preferred_element_type=F32,
        )
        total[...] += sums[0:VEL] + sums[VEL : 2 * VEL] + sums[2 * VEL :]
        if c == CHUNKS - 1:
            for i in range(VEL):
                part[i] = total[i : i + 1]

            def give(owner):
                pltpu.make_async_remote_copy(
                    src_ref=part.at[owner], dst_ref=part_in.at[v], send_sem=psend_sem, recv_sem=precv_sem,
                    device_id={"vel": owner}, device_id_type=MESH,
                ).start()

            def give_next(k, _):
                o = (k * STRIDE) & (VEL - 1)
                give(device((o >> 1) & 3, o >> 3, o & 1))
                return 0

            lax.fori_loop(1, VEL, give_next, 0)

        moments = (fluid * relax_c) * ((first - wall * second) / total_weight)
        high, low = split(moments)
        stacked = jnp.concatenate([high, high, low, low], axis=0)
        keep = fluid * (1.0 - relax_c)
        keep_wall = keep * wall
        def rows_of(r, _):
            rows = pl.ds(pl.multiple_of(r * ROWS, ROWS), ROWS)
            collided = jnp.dot(btab[rows, 0:64], stacked, preferred_element_type=F32)
            for j in range(WIDTH // 128):
                sub = slice(j * 128, (j + 1) * 128)
                at = pl.ds(pl.multiple_of(c * WIDTH + j * 128, 128), 128)
                factor = keep[:, sub] - keep_wall[:, sub] * absorb_tab[rows, :]
                value = factor * mu[rows, at].astype(F32) + collided[:, sub]
                result[rows, at] = value.astype(BF16)
            return 0

        lax.fori_loop(0, Q // ROWS, rows_of, 0)
        return 0

    for c in range(CHUNKS):
        collide(c, 0)

    part_in[pl.ds(v, 1)] = part[pl.ds(v, 1)]
    sent = part.at[pl.ds(0, VEL - 1)]
    pltpu.make_async_copy(sent, sent, precv_sem).wait()
    grad = part_in[0]
    for i in range(1, VEL):
        grad = grad + part_in[i]
    grad_out[...] = grad

    pltpu.make_async_copy(sent, sent, psend_sem).wait()
    staged_out = staged.at[pl.ds(0, VEL - 1)]
    pltpu.make_async_copy(staged_out, staged_out, send_sem).wait()

    @pl.when(g > 0)
    def _():
        to_lower().wait_send()

    @pl.when(g < GRP - 1)
    def _():
        to_upper().wait_send()


def store_kernel(result, grad, out_hbm, grad_hbm, small, out_sem, grad_sem):
    copies = []
    for c in range(STORES):
        rows = pl.ds(c * (Q // STORES), Q // STORES)
        copies.append(pltpu.make_async_copy(result.at[rows], out_hbm.at[rows], out_sem.at[c]))
    for copy in copies:
        copy.start()
    small[...] = grad[:, 0:PATCH_DEV]
    last = pltpu.make_async_copy(small, grad_hbm, grad_sem)
    last.start()
    for copy in copies:
        copy.wait()
    last.wait()


def in_hbm(x):
    return pltpu.with_memory_space_constraint(x, pltpu.HBM)


def in_vmem(x):
    return pltpu.with_memory_space_constraint(x, pltpu.VMEM)


def body(adjoint, relaxation, reaction, base_moments, cell_kind, patch_id):
    dma = pltpu.SemaphoreType.DMA
    hbm = pl.BlockSpec(memory_space=pltpu.HBM)
    vmem = pl.BlockSpec(memory_space=pltpu.VMEM)
    result, grad = pl.pallas_call(
        kernel,
        out_shape=(pltpu.VMEM((Q, CELLS), BF16), pltpu.VMEM((1, 128), F32)),
        in_specs=[hbm] * 6,
        out_specs=(vmem, vmem),
        scratch_shapes=[
            pltpu.VMEM((LOCAL, XB, CELLS), BF16),
            pltpu.VMEM((XB + 2, LOCAL, CELLS), BF16),
            pltpu.VMEM((XB, LOCAL, CELLS), BF16),
            pltpu.VMEM((Q, CELLS), BF16),
            pltpu.VMEM((1, CELLS), F32),
            pltpu.VMEM((1, CELLS), F32),
            pltpu.VMEM((MOMENTS, 1, CELLS), F32),
            pltpu.VMEM((1, CELLS), jnp.int32),
            pltpu.VMEM((1, CELLS), jnp.int32),
            pltpu.VMEM((Q, 128), F32),
            pltpu.VMEM((64, Q), BF16),
            pltpu.VMEM((Q, 128), BF16),
            pltpu.VMEM((VEL, 1, 128), F32),
            pltpu.VMEM((VEL, 1, 128), F32),
            pltpu.VMEM((VEL, 128), F32),
            pltpu.VMEM((16, CELLS), F32),
            pltpu.VMEM((128, CELLS), BF16),
            pltpu.SemaphoreType.REGULAR,
            dma((CHUNKS,)),
            dma((5,)),
            dma((2,)),
            dma((2,)),
            dma,
            dma((CHUNKS,)),
            dma,
            dma,
        ],
        compiler_params=pltpu.CompilerParams(
            collective_id=0, has_side_effects=True, vmem_limit_bytes=40 * 1024 * 1024
        ),
        name="adjoint_step",
    )(*[in_hbm(x) for x in (adjoint, relaxation, reaction, base_moments, cell_kind, patch_id)])
    out, grad = pl.pallas_call(
        store_kernel,
        out_shape=(jax.ShapeDtypeStruct((Q, CELLS), BF16), jax.ShapeDtypeStruct((1, PATCH_DEV), F32)),
        in_specs=[vmem] * 2,
        out_specs=(hbm, hbm),
        scratch_shapes=[pltpu.VMEM((1, PATCH_DEV), F32), dma((STORES,)), dma],
        compiler_params=pltpu.CompilerParams(vmem_limit_bytes=8 * 1024 * 1024),
        name="store_step",
    )(in_vmem(result), in_vmem(grad))
    return out.reshape(Q, 1, 1, CELLS), grad.reshape(PATCH_DEV)


def solution(mesh):
    placed = (
        P("vel", "grp", None, None),
        P("grp", "vel", None),
        P("grp", "vel", None),
        P(None, "grp", "vel", None),
        P("grp", "vel", None),
        P("grp", "vel", None),
    )
    return jax.shard_map(
        body,
        mesh=mesh,
        in_specs=placed,
        out_specs=(P(None, "grp", "vel", None), P(("vel", "grp"))),
        check_vma=False,
    )
```
